256 devices in a mesh: row: 8 (over y_hi, x), col: 32 (over z, y_lo, core).
Axes of the slice: x: 4, y: 4 (y_hi: 2, y_lo: 2; y = y_hi * 2 + y_lo), z: 8, core: 2. Of those that a mesh axis runs over, the one named last changes fastest.
Arguments:
- query_pair: bfloat16 [8, 4096, 128], P('row', 'col'), may hold values from -40 to 40
- key_pair: bfloat16 [8, 4096, 128], P('row', 'col'), may hold values from -4 to 4
- value_pair: bfloat16 [8, 4096, 128], P('row', 'col'), may hold values from -6 to 6
- pair_bias: bfloat16 [4, 4096, 4096], P(None, 'col', 'row'), may hold values from -9 to 9
- residue_mask: int32 [4096], P('row'), may hold values from 0 to 1, as said below
- grad_output: bfloat16 [8, 4096, 128], P('row', 'col'), may hold values from -6 to 6
Outputs:
- grad_query: float32 [8, 4096, 128], P('row', 'col')
- grad_key: float32 [8, 4096, 128], P('row', 'col')
- grad_value: float32 [8, 4096, 128], P('row', 'col')
- grad_bias: float32 [4, 4096, 4096], P(None, 'col', 'row')
The draws below stay inside these ranges and needn't reach their ends.
Inputs may be any that keep to these rules, and one draw needn't show every extreme that they name: `residue_mask`: residue 0 is present.
All inputs are finite; a program needn't handle non-finite values.
Results may differ from the reference program's by a relative error of at most 0.01.
Values may be sent and summed in bfloat16 or wider, within the bound.
A program may use at most 64 MiB of HBM per device.

```python
import math
import jax
import jax.numpy as jnp
from jax import lax

CZ = 128
HEADS = 4
HEAD_DIM = 32
BAND = 8
RESIDUES = 4096


def draw_query_pair(key, part):
    key = jax.random.fold_in(key, 11)
    normal_part = jax.random.normal(key, (BAND, RESIDUES, CZ), jnp.float32)
    return jnp.clip(normal_part, -4.0, 4.0).astype(jnp.bfloat16)


def draw_key_pair(key, part):
    key = jax.random.fold_in(key, 23)
    normal_part = jax.random.normal(key, (BAND, RESIDUES, CZ), jnp.float32)
    return jnp.clip(normal_part, -4.0, 4.0).astype(jnp.bfloat16)


def draw_residue_mask(key, part):
    key = jax.random.fold_in(key, 5)
    levels = jax.random.randint(key, (RESIDUES,), 0, 5)
    present = jnp.where(levels > 0, 1, 0)
    return jnp.where(jnp.arange(RESIDUES) == 0, 1, present).astype(jnp.int32)


def shard_levels(own_key, shape, shards, low, largest):
    gain = 1.0
    for dim, shards_of in shards:
        steps = jax.random.uniform(jax.random.fold_in(jax.random.fold_in(own_key, 6), dim), (shards_of,), jnp.float32, low / len(shards), largest / len(shards))
        gain = gain * jnp.repeat(jnp.exp(steps), shape[dim] // shards_of).reshape((-1,) + (1,) * (len(shape) - 1 - dim))
    return gain


def normal_values(stream_key, shape, scale, reach, split=(), held_as=jnp.bfloat16):
    entries = scale * jax.random.normal(stream_key, shape, jnp.float32)
    if split:
        entries = entries * shard_levels(stream_key, shape, split, -0.22, 0.18)
    return jnp.clip(entries, -reach, reach).astype(held_as)


def setup_inputs(seed: int = 0) -> dict:
    arg_keys = jax.random.split(jax.random.key(seed), 7)
    query_pair = draw_query_pair(jax.random.fold_in(arg_keys[6], 71), 0)
    key_pair = draw_key_pair(jax.random.fold_in(arg_keys[6], 71), 0)
    value_pair = normal_values(arg_keys[2], (BAND, RESIDUES, CZ), 1.0, 6.0, ((0, 8), (1, 32)))
    pair_bias = normal_values(arg_keys[3], (HEADS, RESIDUES, RESIDUES), 1.5, 9.0, ((1, 32), (2, 8)))
    residue_mask = draw_residue_mask(jax.random.fold_in(arg_keys[6], 71), 0)
    grad_output = normal_values(arg_keys[5], (BAND, RESIDUES, CZ), 1.0, 6.0, ((0, 8), (1, 32)))
    return {"query_pair": query_pair, "key_pair": key_pair, "value_pair": value_pair, "pair_bias": pair_bias, "residue_mask": residue_mask, "grad_output": grad_output}


def reference(query_pair, key_pair, value_pair, pair_bias, residue_mask, grad_output):
    score_scale = 1.0 / math.sqrt(HEAD_DIM)
    highest = lax.Precision.HIGHEST
    masked_bias = jnp.where(residue_mask[None, None, :] == 1, pair_bias.astype(jnp.float32), jnp.float32(-1000000000.0))

    def one_row(carried, row_data):
        query_row, key_row, value_row, grad_row = row_data
        query_heads = query_row.astype(jnp.float32).reshape(RESIDUES, HEADS, HEAD_DIM)
        key_heads = key_row.astype(jnp.float32).reshape(RESIDUES, HEADS, HEAD_DIM)
        value_heads = value_row.astype(jnp.float32).reshape(RESIDUES, HEADS, HEAD_DIM)
        grad_heads = grad_row.astype(jnp.float32).reshape(RESIDUES, HEADS, HEAD_DIM)
        scores = jnp.einsum('jhd,khd->hjk', query_heads, key_heads, precision=highest) * score_scale + masked_bias
        row_max = lax.optimization_barrier(jnp.max(scores, axis=-1, keepdims=True))
        expo = jnp.exp(scores - row_max)
        weights = expo / lax.optimization_barrier(jnp.sum(expo, axis=-1, keepdims=True))
        attended = jnp.einsum('hjk,khd->jhd', weights, value_heads, precision=highest)
        row_delta = lax.optimization_barrier(jnp.sum(grad_heads * attended, axis=-1))
        weight_grad = jnp.einsum('jhd,khd->hjk', grad_heads, value_heads, precision=highest)
        score_grad = weights * (weight_grad - jnp.transpose(row_delta)[:, :, None])
        weights_low = lax.optimization_barrier(weights.astype(jnp.bfloat16)).astype(jnp.float32)
        score_low = lax.optimization_barrier(score_grad.astype(jnp.bfloat16)).astype(jnp.float32)
        grad_q = jnp.einsum('hjk,khd->jhd', score_low, key_heads, precision=highest) * score_scale
        grad_k = jnp.einsum('hjk,jhd->khd', score_low, query_heads, precision=highest) * score_scale
        grad_v = jnp.einsum('hjk,jhd->khd', weights_low, grad_heads, precision=highest)
        outputs = (grad_q.reshape(RESIDUES, CZ), grad_k.reshape(RESIDUES, CZ), grad_v.reshape(RESIDUES, CZ))
        return (carried + score_grad, outputs)
    initial = jnp.zeros((HEADS, RESIDUES, RESIDUES), jnp.float32)
    grad_bias, (grad_query, grad_key, grad_value) = lax.scan(one_row, initial, (query_pair, key_pair, value_pair, grad_output))
    return (grad_query, grad_key, grad_value, grad_bias)
```

```python
import math

import jax
import jax.numpy as jnp
from jax import lax
from jax.experimental import pallas as pl
from jax.experimental.pallas import tpu as pltpu
from jax.sharding import PartitionSpec as P

HEADS = 4
HEAD_DIM = 32
ROWS = 8
PLANES = 8
BLOCK = 128
KEYS = 512
CHANNELS = 128
MESH = pl.DeviceIdType.MESH
LOG2E = 1.4426950408889634
SCALE = 1.0 / math.sqrt(HEAD_DIM)
F32 = jnp.float32
BF16 = jnp.bfloat16
DISTANCES = (1, 7, 2, 6, 3, 5, 4)


def wait_copy(ref, sem):
    pltpu.make_async_copy(ref, ref, sem).wait()


def nt(a, b):
    return lax.dot_general(a, b, (((1,), (1,)), ((), ())), preferred_element_type=F32)


def kernel(
    q_ref, k_ref, v_ref, b_ref, m_ref, g_ref,
    dq_ref, dk_ref, dv_ref, db_ref,
    zbuf, qg, kv, qm, bias_t, db_acc, p_buf, wg_buf, local, st, coef, wl, dl,
    own, cx_out, cx_in, rr_out, rr_in, zr_out, zr_in, zown, dq_out, dq_in,
    z_s, z_r, q_s, q_r, r_s, r_r, e_s, e_r, st_s, st_r, cx_s, cx_r, rr_s, rr_r,
    zr_s, zr_r, dq_s, dq_r,
):
    r = lax.axis_index("row")
    c = lax.axis_index("col")
    z = c // 4
    yl = (c // 2) % 2
    core = c % 2
    other = (r, c + 1 - 2 * core)

    def place(row, plane, y):
        return (row, plane * 4 + y * 2 + core)

    barrier = pltpu.get_barrier_semaphore()

    def greet(target):
        pl.semaphore_signal(barrier, inc=1, device_id=target, device_id_type=MESH)

    greet(other)
    for d in range(1, PLANES):
        greet((r, (c + 4 * d) % 32))
    for d in range(ROWS):
        for y in range(2):
            if d or y:
                greet(place((r + d) % ROWS, z, (yl + y) % 2))
    zbuf[0, z] = k_ref[0]
    zbuf[1, z] = v_ref[0]
    qg[0, r] = q_ref[0]
    qg[1, r] = g_ref[0]
    pl.semaphore_wait(barrier, 23)

    def z_copy(kind, d):
        return pltpu.make_async_remote_copy(
            zbuf.at[kind, z], zbuf.at[kind, z], z_s.at[kind, d], z_r.at[kind, d],
            device_id=(r, (c + 4 * d) % 32), device_id_type=MESH)

    def q_copy(kind, d):
        return pltpu.make_async_remote_copy(
            qg.at[kind, r], qg.at[kind, r], q_s.at[kind, d], q_r.at[kind, d],
            device_id=((r + d) % ROWS, c), device_id_type=MESH)

    for kind in range(2):
        for d in DISTANCES:
            z_copy(kind, d).start()
        for d in range(1, ROWS):
            q_copy(kind, d).start()

    def r_copy(kind, plane, y):
        return pltpu.make_async_remote_copy(
            zbuf.at[kind, plane], kv.at[kind, core, r, yl],
            r_s.at[kind, plane * 2 + y], r_r.at[kind, r * 2 + yl],
            device_id=place(plane, z, y), device_id_type=MESH)

    def spread(kind, d):
        plane = (z + PLANES - d) % PLANES
        if d:
            wait_copy(zbuf.at[kind, plane], z_r.at[kind, d])
        for y in range(2):
            mine = jnp.logical_and(plane == r, y == yl)

            @pl.when(mine)
            def _():
                pltpu.make_async_copy(
                    zbuf.at[kind, plane], kv.at[kind, core, r, yl], r_r.at[kind, r * 2 + yl]
                ).start()

            @pl.when(jnp.logical_not(mine))
            def _():
                r_copy(kind, plane, y).start()

    def e_copy(kind, i):
        return pltpu.make_async_remote_copy(
            kv.at[kind, core, i], kv.at[kind, core, i], e_s.at[kind, i], e_r.at[kind, i],
            device_id=other, device_id_type=MESH)

    def share(kind, i):
        for y in range(2):
            wait_copy(kv.at[kind, core, i, y], r_r.at[kind, i * 2 + y])
        e_copy(kind, i).start()

    spread(0, 0)
    present = m_ref[...] == 1
    for h in range(HEADS):
        masked = jnp.where(present, b_ref[h].astype(F32), -1000000000.0) * LOG2E
        for part in range(4):
            q_index = (part % 2) * 2 + part // 2
            bias_t[h, part * BLOCK:(part + 1) * BLOCK, :] = jnp.transpose(
                masked[:, q_index * BLOCK:(q_index + 1) * BLOCK])
    db_acc[...] = jnp.zeros_like(db_acc)
    for d in DISTANCES:
        spread(0, d)
    spread(1, 0)
    for step in range(ROWS):
        share(0, (r + step) % ROWS)

    lanes = lax.broadcasted_iota(jnp.int32, (BLOCK, CHANNELS), 1) // HEAD_DIM

    def split_heads(kind, i):
        block = qg[kind, i]
        for h in range(HEADS):
            qm[kind, i, h * BLOCK:(h + 1) * BLOCK, :] = jnp.where(lanes == h, block, jnp.zeros_like(block))

    def score_row(i):
        @pl.when(i != r)
        def _():
            wait_copy(qg.at[0, i], q_r.at[0, (r + ROWS - i) % ROWS])
        wait_copy(kv.at[0, 1 - core, i], e_r.at[0, i])
        split_heads(0, i)
        keys = kv[0, :, i].reshape(KEYS, CHANNELS)
        for pair in range(2):
            products = nt(keys, qm[0, i, pair * 256:(pair + 1) * 256, :])
            for half in range(2):
                h = pair * 2 + half
                s = products[:, half * BLOCK:(half + 1) * BLOCK] * (SCALE * LOG2E) + bias_t[h]
                top = jnp.max(s, axis=0, keepdims=True)
                p = jnp.exp2(s - top)
                p_buf[i, h] = p
                local[i, h:h + 1, :] = top
                local[i, HEADS + h:HEADS + h + 1, :] = jnp.sum(p, axis=0, keepdims=True)

    def first(t, carried):
        score_row((r + t) % ROWS)
        return carried

    for d in DISTANCES:
        spread(1, d)
    lax.fori_loop(0, ROWS, first, 0)
    for step in range(ROWS):
        share(1, (r + step) % ROWS)

    def second(t, carried):
        i = (r + t) % ROWS

        @pl.when(i != r)
        def _():
            wait_copy(qg.at[1, i], q_r.at[1, (r + ROWS - i) % ROWS])
        wait_copy(kv.at[1, 1 - core, i], e_r.at[1, i])
        split_heads(1, i)
        values = kv[1, :, i].reshape(KEYS, CHANNELS)
        for pair in range(2):
            products = nt(values, qm[1, i, pair * 256:(pair + 1) * 256, :])
            for half in range(2):
                h = pair * 2 + half
                wg = products[:, half * BLOCK:(half + 1) * BLOCK]
                wg_buf[i, h] = wg
                total = local[i, HEADS + h:HEADS + h + 1, :]
                dot = jnp.sum(p_buf[i, h] * wg, axis=0, keepdims=True)
                st[r, i, h:h + 1, :] = local[i, h:h + 1, :] + jnp.log(total) * LOG2E
                st[r, i, HEADS + h:HEADS + h + 1, :] = dot / total
        return carried

    lax.fori_loop(0, ROWS, second, 0)

    def st_copy(d):
        return pltpu.make_async_remote_copy(
            st.at[r], st.at[r], st_s.at[d], st_r.at[d],
            device_id=((r + d) % ROWS, c), device_id_type=MESH)

    for d in range(1, ROWS):
        st_copy(d).start()
    for d in range(1, ROWS):
        wait_copy(st.at[(r + ROWS - d) % ROWS], st_r.at[d])
    parts = [st[d] for d in range(ROWS)]
    logs = [part[:, :HEADS] for part in parts]
    peak = logs[0]
    for part in logs[1:]:
        peak = jnp.maximum(peak, part)
    shares = [jnp.exp2(part - peak) for part in logs]
    norm = sum(shares[1:], shares[0])
    delta = sum(s * part[:, HEADS:] for s, part in zip(shares, parts)) / norm
    coef[:, :HEADS] = jnp.exp2(local[:, :HEADS] - peak) / norm
    coef[:, HEADS:] = delta

    def cx_copy(t):
        return pltpu.make_async_remote_copy(
            cx_out.at[t], cx_in.at[t], cx_s.at[t], cx_r.at[t],
            device_id=other, device_id_type=MESH)

    def rr_copy(t, y):
        return pltpu.make_async_remote_copy(
            rr_out.at[t, y], rr_in.at[r, yl], rr_s.at[t * 2 + y], rr_r.at[r * 2 + yl],
            device_id=place((r + 1 + t) % ROWS, z, y), device_id_type=MESH)

    def zr_copy(row):
        return pltpu.make_async_remote_copy(
            zr_out.at[row], zr_in.at[z], zr_s.at[row], zr_r.at[z],
            device_id=(r, row * 4 + c % 4), device_id_type=MESH)

    def dq_copy(t):
        return pltpu.make_async_remote_copy(
            dq_out.at[t], dq_in.at[r], dq_s.at[t], dq_r.at[r],
            device_id=((r + 1 + t) % ROWS, c), device_id_type=MESH)

    def grads(t):
        i = (r + 1 + t) % ROWS
        keys = kv[0, :, i].reshape(KEYS, CHANNELS)
        for h in range(HEADS):
            w = p_buf[i, h] * coef[i, h:h + 1, :]
            ds = w * (wg_buf[i, h] - coef[i, HEADS + h:HEADS + h + 1, :])
            db_acc[h] += ds
            wl[:, h * BLOCK:(h + 1) * BLOCK] = w.astype(BF16)
            dl[:, h * BLOCK:(h + 1) * BLOCK] = ds.astype(BF16)
        for kind, grid in ((0, dl), (1, wl)):
            part = jnp.dot(grid[...], qm[kind, i], preferred_element_type=F32)
            part = part.reshape(2, 2, BLOCK, CHANNELS)
            for y in range(2):
                own[t, y, kind] = jnp.where(core == 0, part[0, y], part[1, y])
                cx_out[t, y, kind] = jnp.where(core == 0, part[1, y], part[0, y]).astype(BF16)
        cx_copy(t).start()
        cross = lax.dot_general(keys, dl[...], (((0,), (0,)), ((), ())), preferred_element_type=F32)
        turned = jnp.concatenate(
            [cross[h * HEAD_DIM:(h + 1) * HEAD_DIM, h * BLOCK:(h + 1) * BLOCK] for h in range(HEADS)], axis=0)
        dq_out[t] = jnp.transpose(turned).astype(BF16)

        @pl.when(i != r)
        def _():
            dq_copy(t).start()

    def merge_cores(t):
        wait_copy(cx_in.at[t], cx_r.at[t])
        for y in range(2):
            rr_out[t, y] = (own[t, y] + cx_in[t, y].astype(F32)).astype(BF16)
            mine = jnp.logical_and(t == ROWS - 1, y == yl)

            @pl.when(jnp.logical_not(mine))
            def _():
                rr_copy(t, y).start()

            @pl.when(mine)
            def _():
                pltpu.make_async_copy(rr_out.at[t, y], rr_in.at[r, yl], rr_r.at[r * 2 + yl]).start()

    def merge_pair(t):
        row = (r + 2 * ROWS - 1 - t) % ROWS
        for y in range(2):
            wait_copy(rr_in.at[row, y], rr_r.at[row * 2 + y])
        both = rr_in[row, 0].astype(F32) + rr_in[row, 1].astype(F32)

        @pl.when(row == z)
        def _():
            zown[...] = both

        @pl.when(row != z)
        def _():
            zr_out[row] = both.astype(BF16)
            zr_copy(row).start()

    lag_core, lag_pair = 1, 3

    def third(t, carried):
        @pl.when(t < ROWS)
        def _():
            grads(t)

        @pl.when(jnp.logical_and(t >= lag_core, t < ROWS + lag_core))
        def _():
            merge_cores(t - lag_core)

        @pl.when(t >= lag_pair)
        def _():
            merge_pair(t - lag_pair)
        return carried

    lax.fori_loop(0, ROWS + lag_pair, third, 0)

    for h in range(HEADS):
        for part in range(4):
            q_index = (part % 2) * 2 + part // 2
            db_ref[h, :, q_index * BLOCK:(q_index + 1) * BLOCK] = jnp.transpose(
                db_acc[h, part * BLOCK:(part + 1) * BLOCK, :])

    dq = dq_out[ROWS - 1].astype(F32)
    for d in range(1, ROWS):
        row = (r + d) % ROWS
        wait_copy(dq_in.at[row], dq_r.at[row])
        dq += dq_in[row].astype(F32)
    dq_ref[0] = dq * SCALE

    total = zown[...]
    for d in DISTANCES:
        plane = (z + PLANES - d) % PLANES
        wait_copy(zr_in.at[plane], zr_r.at[plane])
        total += zr_in[plane].astype(F32)
    dk_ref[0] = total[0] * SCALE
    dv_ref[0] = total[1]

    for kind in range(2):
        for d in range(1, 8):
            z_copy(kind, d).wait_send()
            q_copy(kind, d).wait_send()
        for plane in range(PLANES):
            for y in range(2):
                @pl.when(jnp.logical_not(jnp.logical_and(plane == r, y == yl)))
                def _():
                    r_copy(kind, plane, y).wait_send()
        for i in range(ROWS):
            e_copy(kind, i).wait_send()
    for d in range(1, ROWS):
        st_copy(d).wait_send()
    for t in range(ROWS):
        cx_copy(t).wait_send()
        for y in range(2):
            if t < ROWS - 1:
                rr_copy(t, y).wait_send()
            else:
                @pl.when(y != yl)
                def _():
                    rr_copy(t, y).wait_send()
        if t < ROWS - 1:
            dq_copy(t).wait_send()

        @pl.when(t != z)
        def _():
            zr_copy(t).wait_send()


def on_device(query_pair, key_pair, value_pair, pair_bias, residue_mask, grad_output):
    block = (BLOCK, CHANNELS)
    dma = pltpu.SemaphoreType.DMA
    scratch = [
        pltpu.VMEM((2, PLANES) + block, BF16),
        pltpu.VMEM((2, ROWS) + block, BF16),
        pltpu.VMEM((2, 2, ROWS, 2) + block, BF16),
        pltpu.VMEM((2, ROWS, HEADS * BLOCK, CHANNELS), BF16),
        pltpu.VMEM((HEADS, KEYS, BLOCK), F32),
        pltpu.VMEM((HEADS, KEYS, BLOCK), F32),
        pltpu.VMEM((ROWS, HEADS, KEYS, BLOCK), F32),
        pltpu.VMEM((ROWS, HEADS, KEYS, BLOCK), F32),
        pltpu.VMEM((ROWS, 2 * HEADS, BLOCK), F32),
        pltpu.VMEM((ROWS, ROWS, 2 * HEADS, BLOCK), F32),
        pltpu.VMEM((ROWS, 2 * HEADS, BLOCK), F32),
        pltpu.VMEM((KEYS, HEADS * BLOCK), BF16),
        pltpu.VMEM((KEYS, HEADS * BLOCK), BF16),
        pltpu.VMEM((ROWS, 2, 2) + block, F32),
        pltpu.VMEM((ROWS, 2, 2) + block, BF16),
        pltpu.VMEM((ROWS, 2, 2) + block, BF16),
        pltpu.VMEM((ROWS, 2, 2) + block, BF16),
        pltpu.VMEM((ROWS, 2, 2) + block, BF16),
        pltpu.VMEM((ROWS, 2) + block, BF16),
        pltpu.VMEM((PLANES, 2) + block, BF16),
        pltpu.VMEM((2,) + block, F32),
        pltpu.VMEM((ROWS,) + block, BF16),
        pltpu.VMEM((ROWS,) + block, BF16),
        dma((2, 8)), dma((2, 8)), dma((2, 8)), dma((2, 8)),
        dma((2, 16)), dma((2, 16)), dma((2, 8)), dma((2, 8)),
        dma((8,)), dma((8,)), dma((8,)), dma((8,)), dma((16,)), dma((16,)),
        dma((8,)), dma((8,)), dma((8,)), dma((8,)),
    ]
    vmem = pl.BlockSpec(memory_space=pltpu.VMEM)
    shape = jax.ShapeDtypeStruct
    return pl.pallas_call(
        kernel,
        out_shape=(
            shape((1,) + block, F32), shape((1,) + block, F32), shape((1,) + block, F32),
            shape((HEADS, BLOCK, KEYS), F32),
        ),
        in_specs=[vmem] * 6,
        out_specs=(vmem,) * 4,
        scratch_shapes=scratch,
        compiler_params=pltpu.CompilerParams(
            collective_id=0, has_side_effects=True, vmem_limit_bytes=56 * 1024 * 1024),
        cost_estimate=pl.CostEstimate(flops=4_000_000_000, bytes_accessed=3_000_000, transcendentals=2_200_000),
    )(query_pair, key_pair, value_pair, pair_bias, residue_mask.reshape(1, -1), grad_output)


def solution(mesh):
    in_specs = (
        P("row", "col", None),
        P("row", "col", None),
        P("row", "col", None),
        P(None, "col", "row"),
        P("row"),
        P("row", "col", None),
    )
    out_specs = (
        P("row", "col", None),
        P("row", "col", None),
        P("row", "col", None),
        P(None, "col", "row"),
    )
    return jax.shard_map(
        on_device, mesh=mesh, in_specs=in_specs, out_specs=out_specs, check_vma=False
    )
```

```python
import math

import jax
import jax.numpy as jnp
from jax import lax
from jax.experimental import pallas as pl
from jax.experimental.pallas import tpu as pltpu
from jax.sharding import PartitionSpec as P

HEADS = 4
HEAD_DIM = 32
ROWS = 8
PLANES = 8
BLOCK = 128
WIDE = 512
HALF = 256
MESH = pl.DeviceIdType.MESH
LOG2E = 1.4426950408889634
SCALE = 1.0 / math.sqrt(HEAD_DIM)
F32 = jnp.float32
BF16 = jnp.bfloat16
FAR_FIRST = (4, 3, 5, 2, 6, 1, 7, 0)
CHUNKS = 4
LINES = 8
K, Q, V, G = 0, 1, 2, 3


def wait_copy(ref, sem):
    pltpu.make_async_copy(ref, ref, sem).wait()


def tn(a, b):
    return lax.dot_general(a, b, (((0,), (0,)), ((), ())), preferred_element_type=F32)


def nt(a, b):
    return lax.dot_general(a, b, (((1,), (1,)), ((), ())), preferred_element_type=F32)


def flip(block):
    return jnp.transpose(block.astype(F32))


def kernel(
    q_ref, k_ref, v_ref, b_ref, m_ref, g_ref,
    grads_ref, own_ref, rest_ref,
    pack, swap, inb, b_swap, b_full, bias_t, db_acc, p_buf, wg_buf, local, st, coef, wl, dl,
    rr_out, rr_in, zr_in, dq_acc, dq_out, dq_in, fx_out, fx_in, dby_out, dby_in, dbo_out, rest,
    swap_s, swap_r, in_s, in_r, b_s, b_r, st_s, st_r, rr_s, rr_r, zr_s, zr_r, dq_s, dq_r,
    fx_s, fx_r, db_s, db_r,
):
    r = lax.axis_index("row")
    c = lax.axis_index("col")
    z = c // 4
    yl = (c // 2) % 2
    core = c % 2
    head = core * 2 + yl
    other = (r, c + 1 - 2 * core)
    across = (r, c + 2 - 4 * yl)

    def place(row, plane, y):
        return (row, plane * 4 + y * 2 + core)

    def remote(src, dst, send, recv, target):
        return pltpu.make_async_remote_copy(
            src, dst, send, recv, device_id=target, device_id_type=MESH)

    def either(mine, local_copy, remote_copy):
        @pl.when(mine)
        def _():
            local_copy.start()

        @pl.when(jnp.logical_not(mine))
        def _():
            remote_copy.start()

    barrier = pltpu.get_barrier_semaphore()

    def greet(target):
        pl.semaphore_signal(barrier, inc=1, device_id=target, device_id_type=MESH)

    home = z == r
    for i in range(ROWS):
        for y in range(2):
            @pl.when(jnp.logical_not(jnp.logical_and(home, jnp.logical_and(i == r, y == yl))))
            def _():
                greet(place(i, r, y))
    for d in range(ROWS):
        for y in range(2):
            if d or y:
                greet(place((r + d) % ROWS, z, (yl + y) % 2))
    for d in range(1, PLANES):
        greet(place(r, (z + d) % PLANES, yl))
    greet(other)

    for kind, ref in ((K, k_ref), (Q, q_ref), (V, v_ref), (G, g_ref)):
        turned = flip(ref[0]).astype(BF16)
        keep = jnp.where(core == 0, turned[:64], turned[64:])
        give = jnp.where(core == 0, turned[64:], turned[:64])
        for y in range(2):
            pack[kind, y, core] = keep[y * HEAD_DIM:(y + 1) * HEAD_DIM]
            swap[kind, y] = give[y * HEAD_DIM:(y + 1) * HEAD_DIM]
    pl.semaphore_wait(barrier, 39 - home.astype(jnp.int32))

    def swap_copy(kind):
        return remote(swap.at[kind], pack.at[kind, :, core], swap_s.at[kind], swap_r.at[kind], other)

    def bias_core():
        return remote(b_ref.at[pl.ds(2 * (1 - core), 2)], b_swap, b_s.at[0], b_r.at[0], other)

    def bias_near():
        return remote(
            b_ref.at[2 * core + 1 - yl], b_full.at[yl, core], b_s.at[1], b_r.at[1], across)

    def bias_far():
        return remote(
            b_swap.at[1 - yl], b_full.at[yl, 1 - core], b_s.at[2], b_r.at[2], across)

    def kv_copy(kind, plane, y):
        return remote(
            pack.at[kind, y], inb.at[kind, r, yl], in_s.at[kind], in_r.at[kind, r],
            place(z, plane, y))

    def qg_copy(kind, row, y):
        return remote(
            pack.at[kind, y], inb.at[kind, r, yl], in_s.at[kind], in_r.at[kind, r],
            place(row, z, y))

    def keep_copy(kind, y):
        return pltpu.make_async_copy(pack.at[kind, y], inb.at[kind, r, yl], in_r.at[kind, r])

    def send_kv(kind):
        wait_copy(pack.at[kind, :, 1 - core], swap_r.at[kind])
        for d in FAR_FIRST:
            plane = (z + d) % PLANES
            for y in range(2):
                if d:
                    kv_copy(kind, plane, y).start()
                else:
                    either(jnp.logical_and(home, y == yl), keep_copy(kind, y), kv_copy(kind, plane, y))

    def send_qg(kind):
        wait_copy(pack.at[kind, :, 1 - core], swap_r.at[kind])
        for d in FAR_FIRST:
            row = (r + d) % ROWS
            for y in range(2):
                if d:
                    qg_copy(kind, row, y).start()
                else:
                    either(y == yl, keep_copy(kind, y), qg_copy(kind, row, y))

    def drained(kib, sem):
        wait_copy(p_buf.at[0, pl.ds(0, kib // 2)], sem)

    def kv_sent(kind):
        @pl.when(home)
        def _():
            drained(240, in_s.at[kind])

        @pl.when(jnp.logical_not(home))
        def _():
            drained(256, in_s.at[kind])

    swap_copy(K).start()
    bias_near().start()
    bias_core().start()
    for kind in (Q, V, G):
        swap_copy(kind).start()
    send_kv(K)
    wait_copy(b_swap, b_r.at[0])
    bias_far().start()
    send_qg(Q)
    send_kv(V)
    send_qg(G)

    present = m_ref[...] == 1

    def turn_bias(block, y, cc):
        masked = jnp.where(present, block.astype(F32), -1000000000.0) * LOG2E
        start = pl.multiple_of(y * HALF + cc * BLOCK, BLOCK)
        for part in range(4):
            bias_t[part * BLOCK:(part + 1) * BLOCK, pl.ds(start, BLOCK)] = jnp.transpose(
                masked[:, part * BLOCK:(part + 1) * BLOCK])

    turn_bias(b_ref[head], yl, core)
    turn_bias(b_swap[yl], yl, 1 - core)
    db_acc[...] = jnp.zeros_like(db_acc)
    dq_acc[...] = jnp.zeros_like(dq_acc)
    wait_copy(b_full.at[1 - yl, core], b_r.at[1])
    turn_bias(b_full[1 - yl, core], 1 - yl, core)
    wait_copy(b_full.at[1 - yl, 1 - core], b_r.at[2])
    turn_bias(b_full[1 - yl, 1 - core], 1 - yl, 1 - core)

    def wide(kind, i):
        return jnp.concatenate([inb[kind, i, y, cc] for y in range(2) for cc in range(2)], axis=1)

    def folded(block):
        return block.reshape(BLOCK // LINES, LINES, HALF)

    def first(t, carried):
        i = (r + t) % ROWS
        wait_copy(inb.at[K, i], in_r.at[K, i])
        wait_copy(inb.at[Q, i], in_r.at[Q, i])
        keys, queries = flip(wide(K, i)).astype(BF16), wide(Q, i)
        for part in range(2):
            cols = slice(part * HALF, (part + 1) * HALF)
            for chunk in range(CHUNKS):
                rows = slice(chunk * BLOCK, (chunk + 1) * BLOCK)
                s = jnp.dot(keys[rows], queries[:, cols], preferred_element_type=F32)
                s = folded(s * (SCALE * LOG2E) + bias_t[rows, cols])
                top = jnp.max(s, axis=0)
                p = jnp.exp2(s - top)
                p_buf[i, rows, cols] = p.reshape(BLOCK, HALF)
                local[0, i, chunk, :, cols] = top
                local[1, i, chunk, :, cols] = jnp.sum(p, axis=0)
        return carried

    lax.fori_loop(0, ROWS, first, 0)

    def st_copy(part, d):
        return remote(
            st.at[part, r], st.at[part, r], st_s.at[part], st_r.at[part],
            place((r + d) % ROWS, z, yl))

    for part in range(2):
        cols = slice(part * HALF, (part + 1) * HALF)

        def second(t, carried):
            i = (r + t) % ROWS
            if part == 0:
                wait_copy(inb.at[V, i], in_r.at[V, i])
                wait_copy(inb.at[G, i], in_r.at[G, i])
            values = flip(wide(V, i)).astype(BF16)
            gradients = jnp.concatenate([inb[G, i, part, cc] for cc in range(2)], axis=1)
            for chunk in range(CHUNKS):
                rows = slice(chunk * BLOCK, (chunk + 1) * BLOCK)
                wg = jnp.dot(values[rows], gradients, preferred_element_type=F32)
                wg_buf[i, rows, cols] = wg
                local[2, i, chunk, :, cols] = jnp.sum(folded(p_buf[i, rows, cols] * wg), axis=0)
            return carried

        lax.fori_loop(0, ROWS, second, 0)
        tops = local[0, :, :, :, cols].reshape(ROWS, CHUNKS * LINES, HALF)
        top = jnp.max(tops, axis=1, keepdims=True)
        scale = jnp.exp2(tops - top)
        total = jnp.sum(scale * local[1, :, :, :, cols].reshape(tops.shape), axis=1)
        dot = jnp.sum(scale * local[2, :, :, :, cols].reshape(tops.shape), axis=1)
        top = top.reshape(ROWS, HALF)
        st[part, r, 0] = top + jnp.log(total) * LOG2E
        st[part, r, 1] = dot / total
        for d in FAR_FIRST[:-1]:
            st_copy(part, d).start()

    for part in range(2):
        cols = slice(part * HALF, (part + 1) * HALF)
        wait_copy(st.at[part, pl.ds(0, ROWS - 1)], st_r.at[part])
        peak = st[part, 0, 0]
        for d in range(1, ROWS):
            peak = jnp.maximum(peak, st[part, d, 0])
        norm = jnp.zeros_like(peak)
        delta = jnp.zeros_like(peak)
        for d in range(ROWS):
            part_of = jnp.exp2(st[part, d, 0] - peak)
            norm += part_of
            delta += part_of * st[part, d, 1]
        inverse = 1.0 / norm
        delta = delta * inverse
        for i in range(ROWS):
            for chunk in range(CHUNKS):
                coef[i, chunk, :, cols] = jnp.exp2(local[0, i, chunk, :, cols] - peak[i:i + 1]) * inverse[i:i + 1]
            coef[i, CHUNKS, :, cols] = jnp.broadcast_to(delta[i:i + 1], (LINES, HALF))

    def rr_copy(s, t, half):
        return remote(
            rr_out.at[s * 8 + t], rr_in.at[r, yl], rr_s, rr_r.at[r * 2 + yl],
            place((r + 1 + t) % ROWS, z, half))

    def zr_copy(row, hl):
        return remote(
            rr_in.at[row, hl], zr_in.at[z, hl], zr_s, zr_r.at[z],
            place(r, row, yl))

    def dq_copy(t, y):
        return remote(
            dq_out.at[t * 2 + y], dq_in.at[r, yl], dq_s, dq_r,
            place((r + 1 + t) % ROWS, z, y))

    def third(s):
        half = (yl + s) % 2
        rows = pl.ds(pl.multiple_of(half * HALF, HALF), HALF)

        def step(t, carried):
            i = (r + 1 + t) % ROWS
            for part in range(2):
                cols = slice(part * HALF, (part + 1) * HALF)
                delta = coef[i, CHUNKS, :, cols]
                for sub in range(2):
                    rows = pl.ds(pl.multiple_of(half * HALF + sub * BLOCK, BLOCK), BLOCK)
                    out = slice(sub * BLOCK, (sub + 1) * BLOCK)
                    w = folded(p_buf[i, rows, cols]) * coef[i, half * 2 + sub, :, cols]
                    ds = (w * (folded(wg_buf[i, rows, cols]) - delta)).reshape(BLOCK, HALF)
                    w = w.reshape(BLOCK, HALF)
                    db_acc[rows, cols] += ds
                    wl[out, cols] = w.astype(BF16)
                    dl[out, cols] = ds.astype(BF16)
            rr_out[s * 8 + t, 0] = nt(wide(Q, i), dl[...]).astype(BF16)
            rr_out[s * 8 + t, 1] = nt(wide(G, i), wl[...]).astype(BF16)
            mine = jnp.logical_and(t == ROWS - 1, half == yl)
            either(
                mine,
                pltpu.make_async_copy(rr_out.at[s * 8 + t], rr_in.at[r, yl], rr_r.at[r * 2 + yl]),
                rr_copy(s, t, half))
            keys = jnp.concatenate([inb[K, i, half, cc] for cc in range(2)], axis=1)
            total = dq_acc[i] + jnp.dot(keys, dl[...], preferred_element_type=F32)
            if s == 0:
                dq_acc[i] = total
            else:
                for y in range(2):
                    dq_out[t * 2 + y] = total[:, y * HALF:(y + 1) * HALF].astype(BF16)
                    either(
                        jnp.logical_and(t == ROWS - 1, y == yl),
                        pltpu.make_async_copy(dq_out.at[t * 2 + y], dq_in.at[r, yl], dq_r),
                        dq_copy(t, y))
            return carried

        lax.fori_loop(0, ROWS, step, 0)
        away = pl.ds(pl.multiple_of((1 - yl) * HALF, HALF), HALF)
        turned = flip(db_acc[rows, away]).astype(BF16)
        for cc in range(2):
            dby_out[s, cc] = turned[cc * BLOCK:(cc + 1) * BLOCK]
        dby_copy(s, half).start()

    def dby_copy(s, half):
        return remote(dby_out.at[s], dby_in.at[half], db_s.at[s], db_r.at[half], across)

    third(0)
    third(1)

    def forward(u, carried):
        s, t = u // 8, u % 8
        row = (r + 2 * ROWS - 1 - t) % ROWS
        hl = (yl + s) % 2
        wait_copy(rr_in.at[row, hl], rr_r.at[row * 2 + hl])

        @pl.when(row != z)
        def _():
            zr_copy(row, hl).start()
        return carried

    lax.fori_loop(0, 16, forward, 0)

    near = pl.ds(pl.multiple_of(yl * HALF + core * BLOCK, BLOCK), BLOCK)
    far = pl.ds(pl.multiple_of(yl * HALF + (1 - core) * BLOCK, BLOCK), BLOCK)
    turned = flip(db_acc[:, far]).astype(BF16)
    for half in range(2):
        dbo_out[half] = turned[:, half * HALF:(half + 1) * HALF]
    twin = core * 2 + 1 - yl

    def dbo_copy():
        return remote(dbo_out, rest.at[head], db_s.at[2], db_r.at[2], other)

    def dbt_copy(half):
        return remote(
            dby_in.at[half, 1 - core], rest.at[twin, half], db_s.at[3 + half], db_r.at[3 + half], other)

    dbo_copy().start()
    own_ref[...] = flip(db_acc[:, near])
    for s in range(2):
        half = (yl + 1 + s) % 2
        wait_copy(dby_in.at[half], db_r.at[half])
        dbt_copy(half).start()

    total = jnp.zeros((2, HEAD_DIM, HALF), F32)
    wait_copy(dq_in, dq_r)
    for row in range(ROWS):
        total += dq_in[row].astype(F32)

    def hand_over(slot, total):
        low, high = total[:, :, :BLOCK], total[:, :, BLOCK:]
        mine = jnp.where(core == 0, low, high)
        fx_out[slot] = jnp.where(core == 0, high, low)
        grads_ref[slot, core] = mine

    def fx_copy(start, size):
        part = pl.ds(start, size)
        return remote(fx_out.at[part], fx_in.at[part], fx_s.at[start], fx_r.at[start], other)

    hand_over(0, total)
    fx_copy(0, 1).start()

    rest_ref[twin] = dby_in[:, core]
    wait_copy(rest.at[2 * (1 - core) + yl], db_r.at[2])
    for half in range(2):
        wait_copy(rest.at[2 * (1 - core) + 1 - yl, half], db_r.at[3 + half])
    for y in range(2):
        rest_ref[2 * (1 - core) + y] = rest[2 * (1 - core) + y]
    rest_ref[head] = jnp.zeros((2, BLOCK, HALF), BF16)
    wait_copy(fx_in.at[pl.ds(0, 1)], fx_r.at[0])
    grads_ref[0, 1 - core] = fx_in[0]

    total = rr_in[z].astype(F32)
    for d in (1, 7, 2, 6, 3, 5, 4):
        plane = (z + d) % PLANES
        wait_copy(zr_in.at[plane], zr_r.at[plane])
        total += zr_in[plane].astype(F32)
    hand_over(1, total[:, 0])
    hand_over(2, total[:, 1])
    fx_copy(1, 2).start()

    for kind in (K, Q, V, G):
        swap_copy(kind).wait_send()
        if kind in (Q, G):
            drained(240, in_s.at[kind])
        else:
            kv_sent(kind)
    bias_core().wait_send()
    bias_near().wait_send()
    bias_far().wait_send()
    for part in range(2):
        wait_copy(st.at[part, pl.ds(0, ROWS - 1)], st_s.at[part])
    drained(480, rr_s)
    drained(448, zr_s)
    drained(240, dq_s)
    for s in range(2):
        dby_copy(s, (yl + s) % 2).wait_send()
        dbt_copy(s).wait_send()
    dbo_copy().wait_send()
    fx_copy(0, 1).wait_send()
    fx_copy(1, 2).wait_send()
    wait_copy(fx_in.at[pl.ds(1, 2)], fx_r.at[1])
    for slot in (1, 2):
        grads_ref[slot, 1 - core] = fx_in[slot]


def finish(grads_ref, own_ref, rest_ref, dq_ref, dk_ref, dv_ref, db_ref):
    c = lax.axis_index("col")
    head = (c % 2) * 2 + (c // 2) % 2
    for slot, ref, scale in ((0, dq_ref, SCALE), (1, dk_ref, SCALE), (2, dv_ref, None)):
        turned = jnp.transpose(grads_ref[slot].reshape(BLOCK, BLOCK))
        ref[0] = turned if scale is None else turned * scale
    for h in range(HEADS):
        for half in range(2):
            db_ref[h, :, half * HALF:(half + 1) * HALF] = rest_ref[h, half].astype(F32)
    db_ref[head] = own_ref[...]


def on_device(query_pair, key_pair, value_pair, pair_bias, residue_mask, grad_output):
    dma = pltpu.SemaphoreType.DMA
    vm = pltpu.VMEM
    scratch = [
        vm((4, 2, 2, HEAD_DIM, BLOCK), BF16),
        vm((4, 2, HEAD_DIM, BLOCK), BF16),
        vm((4, ROWS, 2, 2, HEAD_DIM, BLOCK), BF16),
        vm((2, BLOCK, WIDE), BF16),
        vm((2, 2, BLOCK, WIDE), BF16),
        vm((WIDE, WIDE), F32),
        vm((WIDE, WIDE), F32),
        vm((ROWS, WIDE, WIDE), F32),
        vm((ROWS, WIDE, WIDE), F32),
        vm((3, ROWS, CHUNKS, LINES, WIDE), F32),
        vm((2, ROWS, 2, ROWS, HALF), F32),
        vm((ROWS, CHUNKS + 1, LINES, WIDE), F32),
        vm((HALF, WIDE), BF16),
        vm((HALF, WIDE), BF16),
        vm((2 * ROWS, 2, HEAD_DIM, HALF), BF16),
        vm((ROWS, 2, 2, HEAD_DIM, HALF), BF16),
        vm((PLANES, 2, 2, HEAD_DIM, HALF), BF16),
        vm((ROWS, HEAD_DIM, WIDE), F32),
        vm((2 * ROWS, HEAD_DIM, HALF), BF16),
        vm((ROWS, 2, HEAD_DIM, HALF), BF16),
        vm((3, 2, HEAD_DIM, BLOCK), F32),
        vm((3, 2, HEAD_DIM, BLOCK), F32),
        vm((2, 2, BLOCK, HALF), BF16),
        vm((2, 2, BLOCK, HALF), BF16),
        vm((2, BLOCK, HALF), BF16),
        vm((HEADS, 2, BLOCK, HALF), BF16),
        dma((4,)), dma((4,)), dma((4,)), dma((4, 8)), dma((3,)), dma((3,)),
        dma((2,)), dma((2,)), dma, dma((16,)), dma, dma((8,)),
        dma, dma, dma((2,)), dma((2,)), dma((5,)), dma((5,)),
    ]
    vmem = pl.BlockSpec(memory_space=pltpu.VMEM)
    shape = jax.ShapeDtypeStruct
    parts = pl.pallas_call(
        kernel,
        out_shape=(
            shape((3, 2, 2, HEAD_DIM, BLOCK), F32),
            shape((BLOCK, WIDE), F32),
            shape((HEADS, 2, BLOCK, HALF), BF16),
        ),
        in_specs=[vmem] * 6,
        out_specs=(vmem,) * 3,
        scratch_shapes=scratch,
        compiler_params=pltpu.CompilerParams(
            collective_id=0, has_side_effects=True, vmem_limit_bytes=56 * 1024 * 1024),
        cost_estimate=pl.CostEstimate(flops=4_000_000_000, bytes_accessed=3_000_000, transcendentals=2_200_000),
    )(query_pair, key_pair, value_pair, pair_bias, residue_mask.reshape(1, -1), grad_output)
    pair = shape((1, BLOCK, BLOCK), F32)
    return pl.pallas_call(
        finish,
        out_shape=(pair, pair, pair, shape((HEADS, BLOCK, WIDE), F32)),
        in_specs=[vmem] * 3,
        out_specs=(vmem,) * 4,
        compiler_params=pltpu.CompilerParams(vmem_limit_bytes=60 * 1024 * 1024),
        cost_estimate=pl.CostEstimate(flops=1_000_000, bytes_accessed=2_500_000, transcendentals=0),
    )(*parts)


def solution(mesh):
    in_specs = (
        P("row", "col", None),
        P("row", "col", None),
        P("row", "col", None),
        P(None, "col", "row"),
        P("row"),
        P("row", "col", None),
    )
    out_specs = (
        P("row", "col", None),
        P("row", "col", None),
        P("row", "col", None),
        P(None, "col", "row"),
    )
    return jax.shard_map(
        on_device, mesh=mesh, in_specs=in_specs, out_specs=out_specs, check_vma=False
    )
```

```python
import math

import jax
import jax.numpy as jnp
from jax import lax
from jax.experimental import pallas as pl
from jax.experimental.pallas import tpu as pltpu
from jax.sharding import PartitionSpec as P

HEADS = 4
HEAD_DIM = 32
ROWS = 8
PLANES = 8
BLOCK = 128
WIDE = 512
HALF = 256
MESH = pl.DeviceIdType.MESH
LOG2E = 1.4426950408889634
SCALE = 1.0 / math.sqrt(HEAD_DIM)
F32 = jnp.float32
BF16 = jnp.bfloat16
FAR_FIRST = (4, 3, 5, 2, 6, 1, 7, 0)
CHUNKS = 4
LINES = 8
K, Q, V, G = 0, 1, 2, 3


def wait_copy(ref, sem):
    pltpu.make_async_copy(ref, ref, sem).wait()


def tn(a, b):
    return lax.dot_general(a, b, (((0,), (0,)), ((), ())), preferred_element_type=F32)


def nt(a, b):
    return lax.dot_general(a, b, (((1,), (1,)), ((), ())), preferred_element_type=F32)


def flip(block):
    return jnp.transpose(block.astype(F32))


def kernel(
    q_ref, k_ref, v_ref, b_ref, m_ref, g_ref,
    grads_ref, own_ref, rest_ref,
    pack, swap, inb, flipped, b_swap, b_full, bias_t, db_acc, p_buf, wg_buf, local, st, coef, wl, dl,
    rr_out, rr_in, zr_in, dq_acc, dq_out, dq_in, fx_out, fx_in, dby_out, dby_in, dbo_out, rest,
    swap_s, swap_r, in_s, in_r, tree_s, b_s, b_r, st_s, st_r, rr_s, rr_r, zr_s, zr_r, dq_s, dq_r,
    fx_s, fx_r, db_s, db_r,
):
    r = lax.axis_index("row")
    c = lax.axis_index("col")
    z = c // 4
    yl = (c // 2) % 2
    core = c % 2
    head = core * 2 + yl
    other = (r, c + 1 - 2 * core)
    across = (r, c + 2 - 4 * yl)

    def place(row, plane, y):
        return (row, plane * 4 + y * 2 + core)

    def remote(src, dst, send, recv, target):
        return pltpu.make_async_remote_copy(
            src, dst, send, recv, device_id=target, device_id_type=MESH)

    def either(mine, local_copy, remote_copy):
        @pl.when(mine)
        def _():
            local_copy.start()

        @pl.when(jnp.logical_not(mine))
        def _():
            remote_copy.start()

    barrier = pltpu.get_barrier_semaphore()

    def greet(target):
        pl.semaphore_signal(barrier, inc=1, device_id=target, device_id_type=MESH)

    home = z == r
    for i in range(ROWS):
        for y in range(2):
            @pl.when(jnp.logical_not(jnp.logical_and(home, jnp.logical_and(i == r, y == yl))))
            def _():
                greet(place(i, r, y))
    for d in range(ROWS):
        for y in range(2):
            if d or y:
                greet(place((r + d) % ROWS, z, (yl + y) % 2))
    for d in range(1, PLANES):
        greet(place(r, (z + d) % PLANES, yl))
    greet(other)

    for kind, ref in ((K, k_ref), (Q, q_ref), (V, v_ref), (G, g_ref)):
        turned = flip(ref[0]).astype(BF16)
        keep = jnp.where(core == 0, turned[:64], turned[64:])
        give = jnp.where(core == 0, turned[64:], turned[:64])
        for y in range(2):
            pack[kind, y, core] = keep[y * HEAD_DIM:(y + 1) * HEAD_DIM]
            swap[kind, y] = give[y * HEAD_DIM:(y + 1) * HEAD_DIM]
    pl.semaphore_wait(barrier, 39 - home.astype(jnp.int32))

    def swap_copy(kind):
        return remote(swap.at[kind], pack.at[kind, :, core], swap_s.at[kind], swap_r.at[kind], other)

    def bias_core():
        return remote(b_ref.at[pl.ds(2 * (1 - core), 2)], b_swap, b_s.at[0], b_r.at[0], other)

    def bias_near():
        return remote(
            b_ref.at[2 * core + 1 - yl], b_full.at[yl, core], b_s.at[1], b_r.at[1], across)

    def bias_far():
        return remote(
            b_swap.at[1 - yl], b_full.at[yl, 1 - core], b_s.at[2], b_r.at[2], across)

    def kv_copy(kind, plane, y):
        return remote(
            pack.at[kind, y], inb.at[kind, r, yl], in_s.at[kind], in_r.at[kind, r],
            place(z, plane, y))

    def qg_copy(kind, row, y):
        return remote(
            pack.at[kind, y], inb.at[kind, r, yl], in_s.at[kind], in_r.at[kind, r],
            place(row, z, y))

    def tree_copy(kind, hi, d):
        i = hi * 4 + r % 4
        return remote(
            inb.at[kind, i], inb.at[kind, i], tree_s.at[kind], in_r.at[kind, i],
            place((r // 4) * 4 + (r + d) % 4, z, yl))

    def tree_qg(kind):
        for step in range(2):
            hi = (r // 4 + step) % 2
            wait_copy(inb.at[kind, hi * 4 + r % 4], in_r.at[kind, hi * 4 + r % 4])
            for d in (2, 1, 3):
                tree_copy(kind, hi, d).start()

    def keep_copy(kind, y):
        return pltpu.make_async_copy(pack.at[kind, y], inb.at[kind, r, yl], in_r.at[kind, r])

    def send_kv(kind):
        wait_copy(pack.at[kind, :, 1 - core], swap_r.at[kind])
        for d in FAR_FIRST:
            plane = (z + d) % PLANES
            for y in range(2):
                if d:
                    kv_copy(kind, plane, y).start()
                else:
                    either(jnp.logical_and(home, y == yl), keep_copy(kind, y), kv_copy(kind, plane, y))

    def send_qg(kind):
        wait_copy(pack.at[kind, :, 1 - core], swap_r.at[kind])
        for d in (4, 0):
            row = (r + d) % ROWS
            for y in range(2):
                if d:
                    qg_copy(kind, row, y).start()
                else:
                    either(y == yl, keep_copy(kind, y), qg_copy(kind, row, y))

    def drained(kib, sem):
        wait_copy(p_buf.at[0, pl.ds(0, kib // 2)], sem)

    def kv_sent(kind):
        @pl.when(home)
        def _():
            drained(240, in_s.at[kind])

        @pl.when(jnp.logical_not(home))
        def _():
            drained(256, in_s.at[kind])

    swap_copy(K).start()
    bias_near().start()
    bias_core().start()
    for kind in (Q, V, G):
        swap_copy(kind).start()
    send_qg(Q)
    send_kv(K)
    send_qg(G)
    wait_copy(b_swap, b_r.at[0])
    bias_far().start()
    send_kv(V)
    tree_qg(Q)
    tree_qg(G)

    present = m_ref[...] == 1

    def turn_bias(block, y, cc):
        masked = jnp.where(present, block.astype(F32), -1000000000.0) * LOG2E
        start = pl.multiple_of(y * HALF + cc * BLOCK, BLOCK)
        for part in range(4):
            bias_t[part * BLOCK:(part + 1) * BLOCK, pl.ds(start, BLOCK)] = jnp.transpose(
                masked[:, part * BLOCK:(part + 1) * BLOCK])

    turn_bias(b_ref[head], yl, core)
    turn_bias(b_swap[yl], yl, 1 - core)
    db_acc[...] = jnp.zeros_like(db_acc)
    dq_acc[...] = jnp.zeros_like(dq_acc)
    wait_copy(b_full.at[1 - yl, core], b_r.at[1])
    turn_bias(b_full[1 - yl, core], 1 - yl, core)
    wait_copy(b_full.at[1 - yl, 1 - core], b_r.at[2])
    turn_bias(b_full[1 - yl, 1 - core], 1 - yl, 1 - core)

    def wide(kind, i):
        return jnp.concatenate([inb[kind, i, y, cc] for y in range(2) for cc in range(2)], axis=1)

    def folded(block):
        return block.reshape(BLOCK // LINES, LINES, HALF)

    def first(t, carried):
        i = (r + t) % ROWS
        wait_copy(inb.at[K, i], in_r.at[K, i])

        @pl.when(i % 4 != r % 4)
        def _():
            wait_copy(inb.at[Q, i], in_r.at[Q, i])
        keys, queries = flip(wide(K, i)).astype(BF16), wide(Q, i)
        for part in range(2):
            cols = slice(part * HALF, (part + 1) * HALF)
            for chunk in range(CHUNKS):
                rows = slice(chunk * BLOCK, (chunk + 1) * BLOCK)
                s = jnp.dot(keys[rows], queries[:, cols], preferred_element_type=F32)
                s = folded(s * (SCALE * LOG2E) + bias_t[rows, cols])
                top = jnp.max(s, axis=0)
                p = jnp.exp2(s - top)
                p_buf[i, rows, cols] = p.reshape(BLOCK, HALF)
                local[0, i, chunk, :, cols] = top
                local[1, i, chunk, :, cols] = jnp.sum(p, axis=0)
        return carried

    lax.fori_loop(0, ROWS, first, 0)

    def st_copy(part, d):
        return remote(
            st.at[part, r], st.at[part, r], st_s.at[part], st_r.at[part],
            place((r + d) % ROWS, z, yl))

    for part in range(2):
        cols = slice(part * HALF, (part + 1) * HALF)

        def second(t, carried):
            i = (r + t) % ROWS
            if part == 0:
                wait_copy(inb.at[V, i], in_r.at[V, i])

                @pl.when(i % 4 != r % 4)
                def _():
                    wait_copy(inb.at[G, i], in_r.at[G, i])
                values = flip(wide(V, i)).astype(BF16)
                flipped[i] = values
            else:
                values = flipped[i]
            gradients = jnp.concatenate([inb[G, i, part, cc] for cc in range(2)], axis=1)
            for chunk in range(CHUNKS):
                rows = slice(chunk * BLOCK, (chunk + 1) * BLOCK)
                wg = jnp.dot(values[rows], gradients, preferred_element_type=F32)
                wg_buf[i, rows, cols] = wg
                local[2, i, chunk, :, cols] = jnp.sum(folded(p_buf[i, rows, cols] * wg), axis=0)
            return carried

        lax.fori_loop(0, ROWS, second, 0)
        tops = local[0, :, :, :, cols].reshape(ROWS, CHUNKS * LINES, HALF)
        top = jnp.max(tops, axis=1, keepdims=True)
        scale = jnp.exp2(tops - top)
        total = jnp.sum(scale * local[1, :, :, :, cols].reshape(tops.shape), axis=1)
        dot = jnp.sum(scale * local[2, :, :, :, cols].reshape(tops.shape), axis=1)
        top = top.reshape(ROWS, HALF)
        st[part, r, 0] = top + jnp.log(total) * LOG2E
        st[part, r, 1] = dot / total
        for d in FAR_FIRST[:-1]:
            st_copy(part, d).start()

    for part in range(2):
        cols = slice(part * HALF, (part + 1) * HALF)
        wait_copy(st.at[part, pl.ds(0, ROWS - 1)], st_r.at[part])
        peak = st[part, 0, 0]
        for d in range(1, ROWS):
            peak = jnp.maximum(peak, st[part, d, 0])
        norm = jnp.zeros_like(peak)
        delta = jnp.zeros_like(peak)
        for d in range(ROWS):
            part_of = jnp.exp2(st[part, d, 0] - peak)
            norm += part_of
            delta += part_of * st[part, d, 1]
        inverse = 1.0 / norm
        delta = delta * inverse
        for i in range(ROWS):
            for chunk in range(CHUNKS):
                coef[i, chunk, :, cols] = jnp.exp2(local[0, i, chunk, :, cols] - peak[i:i + 1]) * inverse[i:i + 1]
            coef[i, CHUNKS, :, cols] = jnp.broadcast_to(delta[i:i + 1], (LINES, HALF))

    def rr_copy(s, t, half):
        return remote(
            rr_out.at[s * 8 + t], rr_in.at[r, yl], rr_s, rr_r.at[r * 2 + yl],
            place((r + z + 1 + t) % ROWS, z, half))

    def zr_copy(row, hl):
        return remote(
            rr_in.at[row, hl], zr_in.at[z, hl], zr_s, zr_r.at[z],
            place(r, row, yl))

    def dq_copy(t, y):
        return remote(
            dq_out.at[t * 2 + y], dq_in.at[r, yl], dq_s, dq_r,
            place((r + z + 1 + t) % ROWS, z, y))

    def third(s):
        half = (yl + s) % 2
        rows = pl.ds(pl.multiple_of(half * HALF, HALF), HALF)

        def step(t, carried):
            i = (r + z + 1 + t) % ROWS
            for part in range(2):
                cols = slice(part * HALF, (part + 1) * HALF)
                delta = coef[i, CHUNKS, :, cols]
                for sub in range(2):
                    rows = pl.ds(pl.multiple_of(half * HALF + sub * BLOCK, BLOCK), BLOCK)
                    out = slice(sub * BLOCK, (sub + 1) * BLOCK)
                    w = folded(p_buf[i, rows, cols]) * coef[i, half * 2 + sub, :, cols]
                    ds = (w * (folded(wg_buf[i, rows, cols]) - delta)).reshape(BLOCK, HALF)
                    w = w.reshape(BLOCK, HALF)
                    db_acc[rows, cols] += ds
                    wl[out, cols] = w.astype(BF16)
                    dl[out, cols] = ds.astype(BF16)
            rr_out[s * 8 + t, 0] = nt(wide(Q, i), dl[...]).astype(BF16)
            rr_out[s * 8 + t, 1] = nt(wide(G, i), wl[...]).astype(BF16)
            mine = jnp.logical_and(i == r, half == yl)
            either(
                mine,
                pltpu.make_async_copy(rr_out.at[s * 8 + t], rr_in.at[r, yl], rr_r.at[r * 2 + yl]),
                rr_copy(s, t, half))
            keys = jnp.concatenate([inb[K, i, half, cc] for cc in range(2)], axis=1)
            total = dq_acc[i] + jnp.dot(keys, dl[...], preferred_element_type=F32)
            if s == 0:
                dq_acc[i] = total
            else:
                for y in range(2):
                    dq_out[t * 2 + y] = total[:, y * HALF:(y + 1) * HALF].astype(BF16)
                    either(
                        jnp.logical_and(i == r, y == yl),
                        pltpu.make_async_copy(dq_out.at[t * 2 + y], dq_in.at[r, yl], dq_r),
                        dq_copy(t, y))
            return carried

        lax.fori_loop(0, ROWS, step, 0)
        away = pl.ds(pl.multiple_of((1 - yl) * HALF, HALF), HALF)
        turned = flip(db_acc[rows, away]).astype(BF16)
        for cc in range(2):
            dby_out[s, cc] = turned[cc * BLOCK:(cc + 1) * BLOCK]
        dby_copy(s, half).start()

    def dby_copy(s, half):
        return remote(dby_out.at[s], dby_in.at[half], db_s.at[s], db_r.at[half], across)

    third(0)
    third(1)

    def forward(u, carried):
        s, t = u // 8, u % 8
        row = (r + 2 * ROWS - z - 1 - t) % ROWS
        hl = (yl + s) % 2
        wait_copy(rr_in.at[row, hl], rr_r.at[row * 2 + hl])

        @pl.when(row != z)
        def _():
            zr_copy(row, hl).start()
        return carried

    lax.fori_loop(0, 16, forward, 0)

    near = pl.ds(pl.multiple_of(yl * HALF + core * BLOCK, BLOCK), BLOCK)
    far = pl.ds(pl.multiple_of(yl * HALF + (1 - core) * BLOCK, BLOCK), BLOCK)
    turned = flip(db_acc[:, far]).astype(BF16)
    for half in range(2):
        dbo_out[half] = turned[:, half * HALF:(half + 1) * HALF]
    twin = core * 2 + 1 - yl

    def dbo_copy():
        return remote(dbo_out, rest.at[head], db_s.at[2], db_r.at[2], other)

    def dbt_copy(half):
        return remote(
            dby_in.at[half, 1 - core], rest.at[twin, half], db_s.at[3 + half], db_r.at[3 + half], other)

    dbo_copy().start()
    own_ref[...] = flip(db_acc[:, near])
    for s in range(2):
        half = (yl + 1 + s) % 2
        wait_copy(dby_in.at[half], db_r.at[half])
        dbt_copy(half).start()

    total = jnp.zeros((2, HEAD_DIM, HALF), F32)
    wait_copy(dq_in, dq_r)
    for row in range(ROWS):
        total += dq_in[row].astype(F32)

    def hand_over(slot, total):
        low, high = total[:, :, :BLOCK], total[:, :, BLOCK:]
        mine = jnp.where(core == 0, low, high)
        fx_out[slot] = jnp.where(core == 0, high, low)
        grads_ref[slot, core] = mine

    def fx_copy(start, size):
        part = pl.ds(start, size)
        return remote(fx_out.at[part], fx_in.at[part], fx_s.at[start], fx_r.at[start], other)

    hand_over(0, total)
    fx_copy(0, 1).start()

    rest_ref[twin] = dby_in[:, core]
    wait_copy(rest.at[2 * (1 - core) + yl], db_r.at[2])
    for half in range(2):
        wait_copy(rest.at[2 * (1 - core) + 1 - yl, half], db_r.at[3 + half])
    for y in range(2):
        rest_ref[2 * (1 - core) + y] = rest[2 * (1 - core) + y]
    rest_ref[head] = jnp.zeros((2, BLOCK, HALF), BF16)
    wait_copy(fx_in.at[pl.ds(0, 1)], fx_r.at[0])
    grads_ref[0, 1 - core] = fx_in[0]

    total = rr_in[z].astype(F32)
    for d in (1, 7, 2, 6, 3, 5, 4):
        plane = (z + d) % PLANES
        wait_copy(zr_in.at[plane], zr_r.at[plane])
        total += zr_in[plane].astype(F32)
    hand_over(1, total[:, 0])
    hand_over(2, total[:, 1])
    fx_copy(1, 2).start()

    for kind in (K, Q, V, G):
        swap_copy(kind).wait_send()
        if kind in (Q, G):
            drained(48, in_s.at[kind])
            drained(192, tree_s.at[kind])
        else:
            kv_sent(kind)
    bias_core().wait_send()
    bias_near().wait_send()
    bias_far().wait_send()
    for part in range(2):
        wait_copy(st.at[part, pl.ds(0, ROWS - 1)], st_s.at[part])
    drained(480, rr_s)
    drained(448, zr_s)
    drained(240, dq_s)
    for s in range(2):
        dby_copy(s, (yl + s) % 2).wait_send()
        dbt_copy(s).wait_send()
    dbo_copy().wait_send()
    fx_copy(0, 1).wait_send()
    fx_copy(1, 2).wait_send()
    wait_copy(fx_in.at[pl.ds(1, 2)], fx_r.at[1])
    for slot in (1, 2):
        grads_ref[slot, 1 - core] = fx_in[slot]


def finish(grads_ref, own_ref, rest_ref, dq_ref, dk_ref, dv_ref, db_ref):
    c = lax.axis_index("col")
    head = (c % 2) * 2 + (c // 2) % 2
    for slot, ref, scale in ((0, dq_ref, SCALE), (1, dk_ref, SCALE), (2, dv_ref, None)):
        turned = jnp.transpose(grads_ref[slot].reshape(BLOCK, BLOCK))
        ref[0] = turned if scale is None else turned * scale
    for h in range(HEADS):
        for half in range(2):
            db_ref[h, :, half * HALF:(half + 1) * HALF] = rest_ref[h, half].astype(F32)
    db_ref[head] = own_ref[...]


def on_device(query_pair, key_pair, value_pair, pair_bias, residue_mask, grad_output):
    dma = pltpu.SemaphoreType.DMA
    vm = pltpu.VMEM
    scratch = [
        vm((4, 2, 2, HEAD_DIM, BLOCK), BF16),
        vm((4, 2, HEAD_DIM, BLOCK), BF16),
        vm((4, ROWS, 2, 2, HEAD_DIM, BLOCK), BF16),
        vm((ROWS, WIDE, HEAD_DIM), BF16),
        vm((2, BLOCK, WIDE), BF16),
        vm((2, 2, BLOCK, WIDE), BF16),
        vm((WIDE, WIDE), F32),
        vm((WIDE, WIDE), F32),
        vm((ROWS, WIDE, WIDE), F32),
        vm((ROWS, WIDE, WIDE), F32),
        vm((3, ROWS, CHUNKS, LINES, WIDE), F32),
        vm((2, ROWS, 2, ROWS, HALF), F32),
        vm((ROWS, CHUNKS + 1, LINES, WIDE), F32),
        vm((HALF, WIDE), BF16),
        vm((HALF, WIDE), BF16),
        vm((2 * ROWS, 2, HEAD_DIM, HALF), BF16),
        vm((ROWS, 2, 2, HEAD_DIM, HALF), BF16),
        vm((PLANES, 2, 2, HEAD_DIM, HALF), BF16),
        vm((ROWS, HEAD_DIM, WIDE), F32),
        vm((2 * ROWS, HEAD_DIM, HALF), BF16),
        vm((ROWS, 2, HEAD_DIM, HALF), BF16),
        vm((3, 2, HEAD_DIM, BLOCK), F32),
        vm((3, 2, HEAD_DIM, BLOCK), F32),
        vm((2, 2, BLOCK, HALF), BF16),
        vm((2, 2, BLOCK, HALF), BF16),
        vm((2, BLOCK, HALF), BF16),
        vm((HEADS, 2, BLOCK, HALF), BF16),
        dma((4,)), dma((4,)), dma((4,)), dma((4, 8)), dma((4,)), dma((3,)), dma((3,)),
        dma((2,)), dma((2,)), dma, dma((16,)), dma, dma((8,)),
        dma, dma, dma((2,)), dma((2,)), dma((5,)), dma((5,)),
    ]
    vmem = pl.BlockSpec(memory_space=pltpu.VMEM)
    shape = jax.ShapeDtypeStruct
    parts = pl.pallas_call(
        kernel,
        out_shape=(
            shape((3, 2, 2, HEAD_DIM, BLOCK), F32),
            shape((BLOCK, WIDE), F32),
            shape((HEADS, 2, BLOCK, HALF), BF16),
        ),
        in_specs=[vmem] * 6,
        out_specs=(vmem,) * 3,
        scratch_shapes=scratch,
        compiler_params=pltpu.CompilerParams(
            collective_id=0, has_side_effects=True, vmem_limit_bytes=56 * 1024 * 1024),
        cost_estimate=pl.CostEstimate(flops=4_000_000_000, bytes_accessed=3_000_000, transcendentals=2_200_000),
    )(query_pair, key_pair, value_pair, pair_bias, residue_mask.reshape(1, -1), grad_output)
    pair = shape((1, BLOCK, BLOCK), F32)
    return pl.pallas_call(
        finish,
        out_shape=(pair, pair, pair, shape((HEADS, BLOCK, WIDE), F32)),
        in_specs=[vmem] * 3,
        out_specs=(vmem,) * 4,
        compiler_params=pltpu.CompilerParams(vmem_limit_bytes=60 * 1024 * 1024),
        cost_estimate=pl.CostEstimate(flops=1_000_000, bytes_accessed=2_500_000, transcendentals=0),
    )(*parts)


def solution(mesh):
    in_specs = (
        P("row", "col", None),
        P("row", "col", None),
        P("row", "col", None),
        P(None, "col", "row"),
        P("row"),
        P("row", "col", None),
    )
    out_specs = (
        P("row", "col", None),
        P("row", "col", None),
        P("row", "col", None),
        P(None, "col", "row"),
    )
    return jax.shard_map(
        on_device, mesh=mesh, in_specs=in_specs, out_specs=out_specs, check_vma=False
    )
```

```python
import math

import jax
import jax.numpy as jnp
from jax import lax
from jax.experimental import pallas as pl
from jax.experimental.pallas import tpu as pltpu
from jax.sharding import PartitionSpec as P

HEADS = 4
HEAD_DIM = 32
ROWS = 8
PLANES = 8
BLOCK = 128
WIDE = 512
HALF = 256
MESH = pl.DeviceIdType.MESH
LOG2E = 1.4426950408889634
SCALE = 1.0 / math.sqrt(HEAD_DIM)
F32 = jnp.float32
BF16 = jnp.bfloat16
FAR_FIRST = (4, 3, 5, 2, 6, 1, 7, 0)
CHUNKS = 4
LINES = 8
K, Q, V, G = 0, 1, 2, 3


def wait_copy(ref, sem):
    pltpu.make_async_copy(ref, ref, sem).wait()


def tn(a, b):
    return lax.dot_general(a, b, (((0,), (0,)), ((), ())), preferred_element_type=F32)


def nt(a, b):
    return lax.dot_general(a, b, (((1,), (1,)), ((), ())), preferred_element_type=F32)


def flip(block):
    return jnp.transpose(block.astype(F32))


def kernel(
    q_ref, k_ref, v_ref, b_ref, m_ref, g_ref,
    grads_ref, own_ref, rest_ref,
    pack, swap, inb, flipped, b_swap, b_full, bias_t, db_acc, p_buf, wg_buf, local, st, coef, wl, dl,
    rr_out, rr_in, zr_in, dq_acc, dq_out, dq_in, fx_out, fx_in, dby_out, dby_in, dbo_out, rest,
    swap_s, swap_r, in_s, in_r, tree_s, b_s, b_r, st_s, st_r, rr_s, rr_r, zr_s, zr_r, dq_s, dq_r,
    fx_s, fx_r, db_s, db_r,
):
    r = lax.axis_index("row")
    c = lax.axis_index("col")
    z = c // 4
    yl = (c // 2) % 2
    core = c % 2
    head = core * 2 + yl
    other = (r, c + 1 - 2 * core)
    across = (r, c + 2 - 4 * yl)

    def place(row, plane, y):
        return (row, plane * 4 + y * 2 + core)

    def remote(src, dst, send, recv, target):
        return pltpu.make_async_remote_copy(
            src, dst, send, recv, device_id=target, device_id_type=MESH)

    def either(mine, local_copy, remote_copy):
        @pl.when(mine)
        def _():
            local_copy.start()

        @pl.when(jnp.logical_not(mine))
        def _():
            remote_copy.start()

    barrier = pltpu.get_barrier_semaphore()

    def greet(target):
        pl.semaphore_signal(barrier, inc=1, device_id=target, device_id_type=MESH)

    home = z == r
    for i in range(ROWS):
        for y in range(2):
            @pl.when(jnp.logical_not(jnp.logical_and(home, jnp.logical_and(i == r, y == yl))))
            def _():
                greet(place(i, r, y))
    for d in range(ROWS):
        for y in range(2):
            if d or y:
                greet(place((r + d) % ROWS, z, (yl + y) % 2))
    for d in range(1, PLANES):
        greet(place(r, (z + d) % PLANES, yl))
    greet(other)

    for kind, ref in ((K, k_ref), (Q, q_ref), (V, v_ref), (G, g_ref)):
        turned = flip(ref[0]).astype(BF16)
        keep = jnp.where(core == 0, turned[:64], turned[64:])
        give = jnp.where(core == 0, turned[64:], turned[:64])
        for y in range(2):
            pack[kind, y, core] = keep[y * HEAD_DIM:(y + 1) * HEAD_DIM]
            swap[kind, y] = give[y * HEAD_DIM:(y + 1) * HEAD_DIM]
    pl.semaphore_wait(barrier, 39 - home.astype(jnp.int32))

    def swap_copy(kind):
        return remote(swap.at[kind], pack.at[kind, :, core], swap_s.at[kind], swap_r.at[kind], other)

    def bias_core():
        return remote(b_ref.at[pl.ds(2 * (1 - core), 2)], b_swap, b_s.at[0], b_r.at[0], other)

    def bias_near():
        return remote(
            b_ref.at[2 * core + 1 - yl], b_full.at[yl, core], b_s.at[1], b_r.at[1], across)

    def bias_far():
        return remote(
            b_swap.at[1 - yl], b_full.at[yl, 1 - core], b_s.at[2], b_r.at[2], across)

    def kv_copy(kind, plane, y):
        return remote(
            pack.at[kind, y], inb.at[kind, r, yl], in_s.at[kind], in_r.at[kind, r],
            place(z, plane, y))

    def qg_copy(kind, row, y):
        return remote(
            pack.at[kind, y], inb.at[kind, r, yl], in_s.at[kind], in_r.at[kind, r],
            place(row, z, y))

    def tree_copy(kind, hi, d):
        i = hi * 4 + r % 4
        return remote(
            inb.at[kind, i], inb.at[kind, i], tree_s.at[kind], in_r.at[kind, i],
            place((r // 4) * 4 + (r + d) % 4, z, yl))

    def tree_qg(kind):
        for step in range(2):
            hi = (r // 4 + step) % 2
            wait_copy(inb.at[kind, hi * 4 + r % 4], in_r.at[kind, hi * 4 + r % 4])
            for d in (2, 1, 3):
                tree_copy(kind, hi, d).start()

    def keep_copy(kind, y):
        return pltpu.make_async_copy(pack.at[kind, y], inb.at[kind, r, yl], in_r.at[kind, r])

    def send_kv(kind):
        wait_copy(pack.at[kind, :, 1 - core], swap_r.at[kind])
        for d in FAR_FIRST:
            plane = (z + d) % PLANES
            for y in range(2):
                if d:
                    kv_copy(kind, plane, y).start()
                else:
                    either(jnp.logical_and(home, y == yl), keep_copy(kind, y), kv_copy(kind, plane, y))

    def send_qg(kind):
        wait_copy(pack.at[kind, :, 1 - core], swap_r.at[kind])
        for d in (4, 0):
            row = (r + d) % ROWS
            for y in range(2):
                if d:
                    qg_copy(kind, row, y).start()
                else:
                    either(y == yl, keep_copy(kind, y), qg_copy(kind, row, y))

    def drained(kib, sem):
        wait_copy(p_buf.at[0, pl.ds(0, kib // 2)], sem)

    def kv_sent(kind):
        @pl.when(home)
        def _():
            drained(240, in_s.at[kind])

        @pl.when(jnp.logical_not(home))
        def _():
            drained(256, in_s.at[kind])

    swap_copy(K).start()
    bias_near().start()
    bias_core().start()
    for kind in (Q, V, G):
        swap_copy(kind).start()
    send_qg(Q)
    send_kv(K)
    send_qg(G)
    wait_copy(b_swap, b_r.at[0])
    bias_far().start()
    send_kv(V)
    tree_qg(Q)
    tree_qg(G)

    present = m_ref[...] == 1

    def turn_bias(block, y, cc):
        masked = jnp.where(present, block.astype(F32), -1000000000.0) * LOG2E
        start = pl.multiple_of(y * HALF + cc * BLOCK, BLOCK)
        for part in range(4):
            bias_t[part * BLOCK:(part + 1) * BLOCK, pl.ds(start, BLOCK)] = jnp.transpose(
                masked[:, part * BLOCK:(part + 1) * BLOCK])

    turn_bias(b_ref[head], yl, core)
    turn_bias(b_swap[yl], yl, 1 - core)
    db_acc[...] = jnp.zeros_like(db_acc)
    dq_acc[...] = jnp.zeros_like(dq_acc)
    wait_copy(b_full.at[1 - yl, core], b_r.at[1])
    turn_bias(b_full[1 - yl, core], 1 - yl, core)
    wait_copy(b_full.at[1 - yl, 1 - core], b_r.at[2])
    turn_bias(b_full[1 - yl, 1 - core], 1 - yl, 1 - core)

    def wide(kind, i):
        return jnp.concatenate([inb[kind, i, y, cc] for y in range(2) for cc in range(2)], axis=1)

    def folded(block):
        return block.reshape(BLOCK // LINES, LINES, HALF)

    def arrive(kv, qg, i):
        wait_copy(inb.at[kv, i], in_r.at[kv, i])

        @pl.when(i % 4 != r % 4)
        def _():
            wait_copy(inb.at[qg, i], in_r.at[qg, i])

    def first(t, carried):
        pair = [(r + 2 * t + step) % ROWS for step in range(2)]
        for i in pair:
            arrive(K, Q, i)
        for i in pair:
            score_row(i)
        return carried

    def score_row(i):
        keys, queries = flip(wide(K, i)).astype(BF16), wide(Q, i)
        for part in range(2):
            cols = slice(part * HALF, (part + 1) * HALF)
            for chunk in range(CHUNKS):
                rows = slice(chunk * BLOCK, (chunk + 1) * BLOCK)
                s = jnp.dot(keys[rows], queries[:, cols], preferred_element_type=F32)
                s = folded(s * (SCALE * LOG2E) + bias_t[rows, cols])
                top = jnp.max(s, axis=0)
                p = jnp.exp2(s - top)
                p_buf[i, rows, cols] = p.reshape(BLOCK, HALF)
                local[0, i, chunk, :, cols] = top
                local[1, i, chunk, :, cols] = jnp.sum(p, axis=0)

    lax.fori_loop(0, ROWS // 2, first, 0)

    def st_copy(part, d):
        return remote(
            st.at[part, r], st.at[part, r], st_s.at[part], st_r.at[part],
            place((r + d) % ROWS, z, yl))

    for part in range(2):
        cols = slice(part * HALF, (part + 1) * HALF)

        def second(t, carried):
            pair = [(r + 2 * t + step) % ROWS for step in range(2)]
            if part == 0:
                for i in pair:
                    arrive(V, G, i)
            for i in pair:
                weight_row(i)
            return carried

        def weight_row(i):
            if part == 0:
                values = flip(wide(V, i)).astype(BF16)
                flipped[i] = values
            else:
                values = flipped[i]
            gradients = jnp.concatenate([inb[G, i, part, cc] for cc in range(2)], axis=1)
            for chunk in range(CHUNKS):
                rows = slice(chunk * BLOCK, (chunk + 1) * BLOCK)
                wg = jnp.dot(values[rows], gradients, preferred_element_type=F32)
                wg_buf[i, rows, cols] = wg
                local[2, i, chunk, :, cols] = jnp.sum(folded(p_buf[i, rows, cols] * wg), axis=0)

        lax.fori_loop(0, ROWS // 2, second, 0)
        tops = local[0, :, :, :, cols].reshape(ROWS, CHUNKS * LINES, HALF)
        top = jnp.max(tops, axis=1, keepdims=True)
        scale = jnp.exp2(tops - top)
        total = jnp.sum(scale * local[1, :, :, :, cols].reshape(tops.shape), axis=1)
        dot = jnp.sum(scale * local[2, :, :, :, cols].reshape(tops.shape), axis=1)
        top = top.reshape(ROWS, HALF)
        st[part, r, 0] = top + jnp.log(total) * LOG2E
        st[part, r, 1] = dot / total
        for d in FAR_FIRST[:-1]:
            st_copy(part, d).start()

    for part in range(2):
        cols = slice(part * HALF, (part + 1) * HALF)
        wait_copy(st.at[part, pl.ds(0, ROWS - 1)], st_r.at[part])
        peak = st[part, 0, 0]
        for d in range(1, ROWS):
            peak = jnp.maximum(peak, st[part, d, 0])
        norm = jnp.zeros_like(peak)
        delta = jnp.zeros_like(peak)
        for d in range(ROWS):
            part_of = jnp.exp2(st[part, d, 0] - peak)
            norm += part_of
            delta += part_of * st[part, d, 1]
        inverse = 1.0 / norm
        delta = delta * inverse
        for i in range(ROWS):
            for chunk in range(CHUNKS):
                coef[i, chunk, :, cols] = jnp.exp2(local[0, i, chunk, :, cols] - peak[i:i + 1]) * inverse[i:i + 1]
            coef[i, CHUNKS, :, cols] = jnp.broadcast_to(delta[i:i + 1], (LINES, HALF))

    def rr_copy(s, t, half):
        return remote(
            rr_out.at[s * 8 + t], rr_in.at[r, yl], rr_s, rr_r.at[r * 2 + yl],
            place((r + z + 1 + t) % ROWS, z, half))

    def zr_copy(row, hl):
        return remote(
            rr_in.at[row, hl], zr_in.at[z, hl], zr_s, zr_r.at[z],
            place(r, row, yl))

    def dq_copy(t, y):
        return remote(
            dq_out.at[t * 2 + y], dq_in.at[r, yl], dq_s, dq_r,
            place((r + z + 1 + t) % ROWS, z, y))

    def third(s):
        half = (yl + s) % 2
        rows = pl.ds(pl.multiple_of(half * HALF, HALF), HALF)

        def weights(t, slot):
            i = (r + z + 1 + t) % ROWS
            for part in range(2):
                cols = slice(part * HALF, (part + 1) * HALF)
                delta = coef[i, CHUNKS, :, cols]
                for sub in range(2):
                    rows = pl.ds(pl.multiple_of(half * HALF + sub * BLOCK, BLOCK), BLOCK)
                    out = slice(sub * BLOCK, (sub + 1) * BLOCK)
                    w = folded(p_buf[i, rows, cols]) * coef[i, half * 2 + sub, :, cols]
                    ds = (w * (folded(wg_buf[i, rows, cols]) - delta)).reshape(BLOCK, HALF)
                    w = w.reshape(BLOCK, HALF)
                    db_acc[rows, cols] += ds
                    wl[slot, out, cols] = w.astype(BF16)
                    dl[slot, out, cols] = ds.astype(BF16)

        def products(t, slot):
            i = (r + z + 1 + t) % ROWS
            rr_out[s * 8 + t, 0] = nt(wide(Q, i), dl[slot]).astype(BF16)
            rr_out[s * 8 + t, 1] = nt(wide(G, i), wl[slot]).astype(BF16)
            keys = jnp.concatenate([inb[K, i, half, cc] for cc in range(2)], axis=1)
            total = dq_acc[i] + jnp.dot(keys, dl[slot], preferred_element_type=F32)
            if s == 0:
                dq_acc[i] = total
            else:
                for y in range(2):
                    dq_out[t * 2 + y] = total[:, y * HALF:(y + 1) * HALF].astype(BF16)

        def send_back(t):
            i = (r + z + 1 + t) % ROWS
            either(
                jnp.logical_and(i == r, half == yl),
                pltpu.make_async_copy(rr_out.at[s * 8 + t], rr_in.at[r, yl], rr_r.at[r * 2 + yl]),
                rr_copy(s, t, half))
            if s:
                for y in range(2):
                    either(
                        jnp.logical_and(i == r, y == yl),
                        pltpu.make_async_copy(dq_out.at[t * 2 + y], dq_in.at[r, yl], dq_r),
                        dq_copy(t, y))

        def step(t, carried):
            weights(2 * t, 0)
            products(2 * t, 0)
            weights(2 * t + 1, 1)
            products(2 * t + 1, 1)
            send_back(2 * t)
            send_back(2 * t + 1)
            return carried

        lax.fori_loop(0, ROWS // 2, step, 0)
        away = pl.ds(pl.multiple_of((1 - yl) * HALF, HALF), HALF)
        turned = flip(db_acc[rows, away]).astype(BF16)
        for cc in range(2):
            dby_out[s, cc] = turned[cc * BLOCK:(cc + 1) * BLOCK]
        dby_copy(s, half).start()

    def dby_copy(s, half):
        return remote(dby_out.at[s], dby_in.at[half], db_s.at[s], db_r.at[half], across)

    third(0)
    third(1)

    def forward(u, carried):
        s, t = u // 8, u % 8
        row = (r + 2 * ROWS - z - 1 - t) % ROWS
        hl = (yl + s) % 2
        wait_copy(rr_in.at[row, hl], rr_r.at[row * 2 + hl])

        @pl.when(row != z)
        def _():
            zr_copy(row, hl).start()
        return carried

    lax.fori_loop(0, 16, forward, 0)

    near = pl.ds(pl.multiple_of(yl * HALF + core * BLOCK, BLOCK), BLOCK)
    far = pl.ds(pl.multiple_of(yl * HALF + (1 - core) * BLOCK, BLOCK), BLOCK)
    turned = flip(db_acc[:, far]).astype(BF16)
    for half in range(2):
        dbo_out[half] = turned[:, half * HALF:(half + 1) * HALF]
    twin = core * 2 + 1 - yl

    def dbo_copy():
        return remote(dbo_out, rest.at[head], db_s.at[2], db_r.at[2], other)

    def dbt_copy(half):
        return remote(
            dby_in.at[half, 1 - core], rest.at[twin, half], db_s.at[3 + half], db_r.at[3 + half], other)

    dbo_copy().start()
    own_ref[...] = flip(db_acc[:, near])
    for s in range(2):
        half = (yl + 1 + s) % 2
        wait_copy(dby_in.at[half], db_r.at[half])
        dbt_copy(half).start()

    total = jnp.zeros((2, HEAD_DIM, HALF), F32)
    wait_copy(dq_in, dq_r)
    for row in range(ROWS):
        total += dq_in[row].astype(F32)

    def hand_over(slot, total):
        low, high = total[:, :, :BLOCK], total[:, :, BLOCK:]
        mine = jnp.where(core == 0, low, high)
        fx_out[slot] = jnp.where(core == 0, high, low)
        grads_ref[slot, core] = mine

    def fx_copy(start, size):
        part = pl.ds(start, size)
        return remote(fx_out.at[part], fx_in.at[part], fx_s.at[start], fx_r.at[start], other)

    hand_over(0, total)
    fx_copy(0, 1).start()

    rest_ref[twin] = dby_in[:, core]
    wait_copy(rest.at[2 * (1 - core) + yl], db_r.at[2])
    for half in range(2):
        wait_copy(rest.at[2 * (1 - core) + 1 - yl, half], db_r.at[3 + half])
    for y in range(2):
        rest_ref[2 * (1 - core) + y] = rest[2 * (1 - core) + y]
    rest_ref[head] = jnp.zeros((2, BLOCK, HALF), BF16)
    wait_copy(fx_in.at[pl.ds(0, 1)], fx_r.at[0])
    grads_ref[0, 1 - core] = fx_in[0]

    total = rr_in[z].astype(F32)
    for d in (1, 7, 2, 6, 3, 5, 4):
        plane = (z + d) % PLANES
        wait_copy(zr_in.at[plane], zr_r.at[plane])
        total += zr_in[plane].astype(F32)
    hand_over(1, total[:, 0])
    hand_over(2, total[:, 1])
    fx_copy(1, 2).start()

    for kind in (K, Q, V, G):
        swap_copy(kind).wait_send()
        if kind in (Q, G):
            drained(48, in_s.at[kind])
            drained(192, tree_s.at[kind])
        else:
            kv_sent(kind)
    bias_core().wait_send()
    bias_near().wait_send()
    bias_far().wait_send()
    for part in range(2):
        wait_copy(st.at[part, pl.ds(0, ROWS - 1)], st_s.at[part])
    drained(480, rr_s)
    drained(448, zr_s)
    drained(240, dq_s)
    for s in range(2):
        dby_copy(s, (yl + s) % 2).wait_send()
        dbt_copy(s).wait_send()
    dbo_copy().wait_send()
    fx_copy(0, 1).wait_send()
    fx_copy(1, 2).wait_send()
    wait_copy(fx_in.at[pl.ds(1, 2)], fx_r.at[1])
    for slot in (1, 2):
        grads_ref[slot, 1 - core] = fx_in[slot]


def finish(grads_ref, own_ref, rest_ref, dq_ref, dk_ref, dv_ref, db_ref):
    c = lax.axis_index("col")
    head = (c % 2) * 2 + (c // 2) % 2
    for slot, ref, scale in ((0, dq_ref, SCALE), (1, dk_ref, SCALE), (2, dv_ref, None)):
        turned = jnp.transpose(grads_ref[slot].reshape(BLOCK, BLOCK))
        ref[0] = turned if scale is None else turned * scale
    for h in range(HEADS):
        for half in range(2):
            db_ref[h, :, half * HALF:(half + 1) * HALF] = rest_ref[h, half].astype(F32)
    db_ref[head] = own_ref[...]


def on_device(query_pair, key_pair, value_pair, pair_bias, residue_mask, grad_output):
    dma = pltpu.SemaphoreType.DMA
    vm = pltpu.VMEM
    scratch = [
        vm((4, 2, 2, HEAD_DIM, BLOCK), BF16),
        vm((4, 2, HEAD_DIM, BLOCK), BF16),
        vm((4, ROWS, 2, 2, HEAD_DIM, BLOCK), BF16),
        vm((ROWS, WIDE, HEAD_DIM), BF16),
        vm((2, BLOCK, WIDE), BF16),
        vm((2, 2, BLOCK, WIDE), BF16),
        vm((WIDE, WIDE), F32),
        vm((WIDE, WIDE), F32),
        vm((ROWS, WIDE, WIDE), F32),
        vm((ROWS, WIDE, WIDE), F32),
        vm((3, ROWS, CHUNKS, LINES, WIDE), F32),
        vm((2, ROWS, 2, ROWS, HALF), F32),
        vm((ROWS, CHUNKS + 1, LINES, WIDE), F32),
        vm((2, HALF, WIDE), BF16),
        vm((2, HALF, WIDE), BF16),
        vm((2 * ROWS, 2, HEAD_DIM, HALF), BF16),
        vm((ROWS, 2, 2, HEAD_DIM, HALF), BF16),
        vm((PLANES, 2, 2, HEAD_DIM, HALF), BF16),
        vm((ROWS, HEAD_DIM, WIDE), F32),
        vm((2 * ROWS, HEAD_DIM, HALF), BF16),
        vm((ROWS, 2, HEAD_DIM, HALF), BF16),
        vm((3, 2, HEAD_DIM, BLOCK), F32),
        vm((3, 2, HEAD_DIM, BLOCK), F32),
        vm((2, 2, BLOCK, HALF), BF16),
        vm((2, 2, BLOCK, HALF), BF16),
        vm((2, BLOCK, HALF), BF16),
        vm((HEADS, 2, BLOCK, HALF), BF16),
        dma((4,)), dma((4,)), dma((4,)), dma((4, 8)), dma((4,)), dma((3,)), dma((3,)),
        dma((2,)), dma((2,)), dma, dma((16,)), dma, dma((8,)),
        dma, dma, dma((2,)), dma((2,)), dma((5,)), dma((5,)),
    ]
    vmem = pl.BlockSpec(memory_space=pltpu.VMEM)
    shape = jax.ShapeDtypeStruct
    parts = pl.pallas_call(
        kernel,
        out_shape=(
            shape((3, 2, 2, HEAD_DIM, BLOCK), F32),
            shape((BLOCK, WIDE), F32),
            shape((HEADS, 2, BLOCK, HALF), BF16),
        ),
        in_specs=[vmem] * 6,
        out_specs=(vmem,) * 3,
        scratch_shapes=scratch,
        compiler_params=pltpu.CompilerParams(
            collective_id=0, has_side_effects=True, vmem_limit_bytes=56 * 1024 * 1024),
        cost_estimate=pl.CostEstimate(flops=4_000_000_000, bytes_accessed=3_000_000, transcendentals=2_200_000),
    )(query_pair, key_pair, value_pair, pair_bias, residue_mask.reshape(1, -1), grad_output)
    pair = shape((1, BLOCK, BLOCK), F32)
    return pl.pallas_call(
        finish,
        out_shape=(pair, pair, pair, shape((HEADS, BLOCK, WIDE), F32)),
        in_specs=[vmem] * 3,
        out_specs=(vmem,) * 4,
        compiler_params=pltpu.CompilerParams(vmem_limit_bytes=60 * 1024 * 1024),
        cost_estimate=pl.CostEstimate(flops=1_000_000, bytes_accessed=2_500_000, transcendentals=0),
    )(*parts)


def solution(mesh):
    in_specs = (
        P("row", "col", None),
        P("row", "col", None),
        P("row", "col", None),
        P(None, "col", "row"),
        P("row"),
        P("row", "col", None),
    )
    out_specs = (
        P("row", "col", None),
        P("row", "col", None),
        P("row", "col", None),
        P(None, "col", "row"),
    )
    return jax.shard_map(
        on_device, mesh=mesh, in_specs=in_specs, out_specs=out_specs, check_vma=False
    )
```

```python
import math

import jax
import jax.numpy as jnp
from jax import lax
from jax.experimental import pallas as pl
from jax.experimental.pallas import tpu as pltpu
from jax.sharding import PartitionSpec as P

HEADS = 4
HEAD_DIM = 32
ROWS = 8
PLANES = 8
BLOCK = 128
WIDE = 512
HALF = 256
MESH = pl.DeviceIdType.MESH
LOG2E = 1.4426950408889634
SCALE = 1.0 / math.sqrt(HEAD_DIM)
F32 = jnp.float32
BF16 = jnp.bfloat16
FAR_FIRST = (4, 3, 5, 2, 6, 1, 7, 0)
CHUNKS = 4
LINES = 8
K, Q, V, G = 0, 1, 2, 3


def wait_copy(ref, sem):
    pltpu.make_async_copy(ref, ref, sem).wait()


def tn(a, b):
    return lax.dot_general(a, b, (((0,), (0,)), ((), ())), preferred_element_type=F32)


def nt(a, b):
    return lax.dot_general(a, b, (((1,), (1,)), ((), ())), preferred_element_type=F32)


def flip(block):
    return jnp.transpose(block.astype(F32))


def kernel(
    q_ref, k_ref, v_ref, b_ref, m_ref, g_ref,
    grads_ref, own_ref, rest_ref,
    pack, swap, inb, flipped, b_swap, b_full, bias_t, db_acc, p_buf, wg_buf, local, st, coef, wl, dl,
    rr_out, rr_in, zr_in, dq_acc, dq_out, dq_in, fx_out, fx_in, dby_out, dby_in, dbo_out, rest,
    swap_s, swap_r, in_s, in_r, tree_s, b_s, b_r, st_s, st_r, rr_s, rr_r, zr_s, zr_r, dq_s, dq_r,
    fx_s, fx_r, db_s, db_r,
):
    r = lax.axis_index("row")
    c = lax.axis_index("col")
    z = c // 4
    yl = (c // 2) % 2
    core = c % 2
    head = core * 2 + yl
    other = (r, c + 1 - 2 * core)
    across = (r, c + 2 - 4 * yl)

    def place(row, plane, y):
        return (row, plane * 4 + y * 2 + core)

    def remote(src, dst, send, recv, target):
        return pltpu.make_async_remote_copy(
            src, dst, send, recv, device_id=target, device_id_type=MESH)

    def either(mine, local_copy, remote_copy):
        @pl.when(mine)
        def _():
            local_copy.start()

        @pl.when(jnp.logical_not(mine))
        def _():
            remote_copy.start()

    barrier = pltpu.get_barrier_semaphore()

    def greet(target):
        pl.semaphore_signal(barrier, inc=1, device_id=target, device_id_type=MESH)

    home = z == r
    for i in range(ROWS):
        for y in range(2):
            @pl.when(jnp.logical_not(jnp.logical_and(home, jnp.logical_and(i == r, y == yl))))
            def _():
                greet(place(i, r, y))
    for d in range(ROWS):
        for y in range(2):
            if d or y:
                greet(place((r + d) % ROWS, z, (yl + y) % 2))
    for d in range(1, PLANES):
        greet(place(r, (z + d) % PLANES, yl))
    greet(other)

    for kind, ref in ((K, k_ref), (Q, q_ref), (V, v_ref), (G, g_ref)):
        turned = flip(ref[0]).astype(BF16)
        keep = jnp.where(core == 0, turned[:64], turned[64:])
        give = jnp.where(core == 0, turned[64:], turned[:64])
        for y in range(2):
            pack[kind, y, core] = keep[y * HEAD_DIM:(y + 1) * HEAD_DIM]
            swap[kind, y] = give[y * HEAD_DIM:(y + 1) * HEAD_DIM]
    pl.semaphore_wait(barrier, 39 - home.astype(jnp.int32))

    def swap_copy(kind):
        return remote(swap.at[kind], pack.at[kind, :, core], swap_s.at[kind], swap_r.at[kind], other)

    def bias_core():
        return remote(b_ref.at[pl.ds(2 * (1 - core), 2)], b_swap, b_s.at[0], b_r.at[0], other)

    def bias_near():
        return remote(
            b_ref.at[2 * core + 1 - yl], b_full.at[yl, core], b_s.at[1], b_r.at[1], across)

    def bias_far():
        return remote(
            b_swap.at[1 - yl], b_full.at[yl, 1 - core], b_s.at[2], b_r.at[2], across)

    def kv_copy(kind, plane, y):
        return remote(
            pack.at[kind, y], inb.at[kind, r, yl], in_s.at[kind], in_r.at[kind, r],
            place(z, plane, y))

    def qg_copy(kind, row, y):
        return remote(
            pack.at[kind, y], inb.at[kind, r, yl], in_s.at[kind], in_r.at[kind, r],
            place(row, z, y))

    def tree_copy(kind, hi, d):
        i = hi * 4 + r % 4
        return remote(
            inb.at[kind, i], inb.at[kind, i], tree_s.at[kind], in_r.at[kind, i],
            place((r // 4) * 4 + (r + d) % 4, z, yl))

    def tree_qg(kind):
        for step in range(2):
            hi = (r // 4 + step) % 2
            wait_copy(inb.at[kind, hi * 4 + r % 4], in_r.at[kind, hi * 4 + r % 4])
            for d in (2, 1, 3):
                tree_copy(kind, hi, d).start()

    def keep_copy(kind, y):
        return pltpu.make_async_copy(pack.at[kind, y], inb.at[kind, r, yl], in_r.at[kind, r])

    def send_kv(kind):
        wait_copy(pack.at[kind, :, 1 - core], swap_r.at[kind])
        for d in FAR_FIRST:
            plane = (z + d) % PLANES
            for y in range(2):
                if d:
                    kv_copy(kind, plane, y).start()
                else:
                    either(jnp.logical_and(home, y == yl), keep_copy(kind, y), kv_copy(kind, plane, y))

    def send_qg(kind):
        wait_copy(pack.at[kind, :, 1 - core], swap_r.at[kind])
        for d in (4, 0):
            row = (r + d) % ROWS
            for y in range(2):
                if d:
                    qg_copy(kind, row, y).start()
                else:
                    either(y == yl, keep_copy(kind, y), qg_copy(kind, row, y))

    def drained(kib, sem):
        wait_copy(p_buf.at[0, pl.ds(0, kib // 2)], sem)

    def kv_sent(kind):
        @pl.when(home)
        def _():
            drained(240, in_s.at[kind])

        @pl.when(jnp.logical_not(home))
        def _():
            drained(256, in_s.at[kind])

    swap_copy(K).start()
    bias_near().start()
    bias_core().start()
    for kind in (Q, V, G):
        swap_copy(kind).start()
    send_qg(Q)
    send_kv(K)
    send_qg(G)
    wait_copy(b_swap, b_r.at[0])
    bias_far().start()
    send_kv(V)
    tree_qg(Q)
    tree_qg(G)

    present = m_ref[...] == 1

    def turn_bias(block, y, cc):
        masked = jnp.where(present, block.astype(F32), -1000000000.0) * LOG2E
        start = pl.multiple_of(y * HALF + cc * BLOCK, BLOCK)
        for part in range(4):
            bias_t[part * BLOCK:(part + 1) * BLOCK, pl.ds(start, BLOCK)] = jnp.transpose(
                masked[:, part * BLOCK:(part + 1) * BLOCK])

    turn_bias(b_ref[head], yl, core)
    turn_bias(b_swap[yl], yl, 1 - core)
    db_acc[...] = jnp.zeros_like(db_acc)
    dq_acc[...] = jnp.zeros_like(dq_acc)
    wait_copy(b_full.at[1 - yl, core], b_r.at[1])
    turn_bias(b_full[1 - yl, core], 1 - yl, core)
    wait_copy(b_full.at[1 - yl, 1 - core], b_r.at[2])
    turn_bias(b_full[1 - yl, 1 - core], 1 - yl, 1 - core)

    def wide(kind, i):
        return jnp.concatenate([inb[kind, i, y, cc] for y in range(2) for cc in range(2)], axis=1)

    def folded(block):
        return block.reshape(BLOCK // LINES, LINES, HALF)

    def arrive(kv, qg, i):
        wait_copy(inb.at[kv, i], in_r.at[kv, i])

        @pl.when(i % 4 != r % 4)
        def _():
            wait_copy(inb.at[qg, i], in_r.at[qg, i])

    def first(t, carried):
        pair = [(r + 4 * t + step) % ROWS for step in range(4)]
        for i in pair:
            arrive(K, Q, i)
        for i in pair:
            score_row(i)
        return carried

    def score_row(i):
        keys, queries = flip(wide(K, i)).astype(BF16), wide(Q, i)
        for part in range(2):
            cols = slice(part * HALF, (part + 1) * HALF)
            for chunk in range(CHUNKS):
                rows = slice(chunk * BLOCK, (chunk + 1) * BLOCK)
                s = jnp.dot(keys[rows], queries[:, cols], preferred_element_type=F32)
                s = folded(s * (SCALE * LOG2E) + bias_t[rows, cols])
                top = jnp.max(s, axis=0)
                p = jnp.exp2(s - top)
                p_buf[i, rows, cols] = p.reshape(BLOCK, HALF)
                local[0, i, chunk, :, cols] = top
                local[1, i, chunk, :, cols] = jnp.sum(p, axis=0)

    lax.fori_loop(0, ROWS // 4, first, 0)

    def st_copy(part, d):
        return remote(
            st.at[part, r], st.at[part, r], st_s.at[part], st_r.at[part],
            place((r + d) % ROWS, z, yl))

    for part in range(2):
        cols = slice(part * HALF, (part + 1) * HALF)

        def second(t, carried):
            pair = [(r + 4 * t + step) % ROWS for step in range(4)]
            if part == 0:
                for i in pair:
                    arrive(V, G, i)
            for i in pair:
                weight_row(i)
            return carried

        def weight_row(i):
            if part == 0:
                values = flip(wide(V, i)).astype(BF16)
                flipped[i] = values
            else:
                values = flipped[i]
            gradients = jnp.concatenate([inb[G, i, part, cc] for cc in range(2)], axis=1)
            for chunk in range(CHUNKS):
                rows = slice(chunk * BLOCK, (chunk + 1) * BLOCK)
                wg = jnp.dot(values[rows], gradients, preferred_element_type=F32)
                wg_buf[i, rows, cols] = wg
                local[2, i, chunk, :, cols] = jnp.sum(folded(p_buf[i, rows, cols] * wg), axis=0)

        lax.fori_loop(0, ROWS // 4, second, 0)
        tops = local[0, :, :, :, cols].reshape(ROWS, CHUNKS * LINES, HALF)
        top = jnp.max(tops, axis=1, keepdims=True)
        scale = jnp.exp2(tops - top)
        total = jnp.sum(scale * local[1, :, :, :, cols].reshape(tops.shape), axis=1)
        dot = jnp.sum(scale * local[2, :, :, :, cols].reshape(tops.shape), axis=1)
        top = top.reshape(ROWS, HALF)
        st[part, r, 0] = top + jnp.log(total) * LOG2E
        st[part, r, 1] = dot / total
        for d in FAR_FIRST[:-1]:
            st_copy(part, d).start()

    for part in range(2):
        cols = slice(part * HALF, (part + 1) * HALF)
        wait_copy(st.at[part, pl.ds(0, ROWS - 1)], st_r.at[part])
        peak = st[part, 0, 0]
        for d in range(1, ROWS):
            peak = jnp.maximum(peak, st[part, d, 0])
        norm = jnp.zeros_like(peak)
        delta = jnp.zeros_like(peak)
        for d in range(ROWS):
            part_of = jnp.exp2(st[part, d, 0] - peak)
            norm += part_of
            delta += part_of * st[part, d, 1]
        inverse = 1.0 / norm
        delta = delta * inverse
        for i in range(ROWS):
            for chunk in range(CHUNKS):
                coef[i, chunk, :, cols] = jnp.exp2(local[0, i, chunk, :, cols] - peak[i:i + 1]) * inverse[i:i + 1]
            coef[i, CHUNKS, :, cols] = jnp.broadcast_to(delta[i:i + 1], (LINES, HALF))

    def rr_copy(s, t, half):
        return remote(
            rr_out.at[s * 8 + t], rr_in.at[r, yl], rr_s, rr_r.at[r * 2 + yl],
            place((r + z + 1 + t) % ROWS, z, half))

    def zr_copy(row, hl):
        return remote(
            rr_in.at[row, hl], zr_in.at[z, hl], zr_s, zr_r.at[z],
            place(r, row, yl))

    def dq_copy(t, y):
        return remote(
            dq_out.at[t * 2 + y], dq_in.at[r, yl], dq_s, dq_r,
            place((r + z + 1 + t) % ROWS, z, y))

    def third(s):
        half = (yl + s) % 2
        rows = pl.ds(pl.multiple_of(half * HALF, HALF), HALF)

        def weights(t, slot):
            i = (r + z + 1 + t) % ROWS
            for part in range(2):
                cols = slice(part * HALF, (part + 1) * HALF)
                delta = coef[i, CHUNKS, :, cols]
                for sub in range(2):
                    rows = pl.ds(pl.multiple_of(half * HALF + sub * BLOCK, BLOCK), BLOCK)
                    out = slice(sub * BLOCK, (sub + 1) * BLOCK)
                    w = folded(p_buf[i, rows, cols]) * coef[i, half * 2 + sub, :, cols]
                    ds = (w * (folded(wg_buf[i, rows, cols]) - delta)).reshape(BLOCK, HALF)
                    w = w.reshape(BLOCK, HALF)
                    db_acc[rows, cols] += ds
                    wl[slot, out, cols] = w.astype(BF16)
                    dl[slot, out, cols] = ds.astype(BF16)

        def products(t, slot):
            i = (r + z + 1 + t) % ROWS
            rr_out[s * 8 + t, 0] = nt(wide(Q, i), dl[slot]).astype(BF16)
            rr_out[s * 8 + t, 1] = nt(wide(G, i), wl[slot]).astype(BF16)
            keys = jnp.concatenate([inb[K, i, half, cc] for cc in range(2)], axis=1)
            total = dq_acc[i] + jnp.dot(keys, dl[slot], preferred_element_type=F32)
            if s == 0:
                dq_acc[i] = total
            else:
                for y in range(2):
                    dq_out[t * 2 + y] = total[:, y * HALF:(y + 1) * HALF].astype(BF16)

        def send_back(t):
            i = (r + z + 1 + t) % ROWS
            either(
                jnp.logical_and(i == r, half == yl),
                pltpu.make_async_copy(rr_out.at[s * 8 + t], rr_in.at[r, yl], rr_r.at[r * 2 + yl]),
                rr_copy(s, t, half))
            if s:
                for y in range(2):
                    either(
                        jnp.logical_and(i == r, y == yl),
                        pltpu.make_async_copy(dq_out.at[t * 2 + y], dq_in.at[r, yl], dq_r),
                        dq_copy(t, y))

        def step(t, carried):
            for pair in range(2):
                u = 4 * t + 2 * pair
                weights(u, 0)
                products(u, 0)
                weights(u + 1, 1)
                products(u + 1, 1)
                send_back(u)
                send_back(u + 1)
            return carried

        lax.fori_loop(0, ROWS // 4, step, 0)
        away = pl.ds(pl.multiple_of((1 - yl) * HALF, HALF), HALF)
        turned = flip(db_acc[rows, away]).astype(BF16)
        for cc in range(2):
            dby_out[s, cc] = turned[cc * BLOCK:(cc + 1) * BLOCK]
        dby_copy(s, half).start()

    def dby_copy(s, half):
        return remote(dby_out.at[s], dby_in.at[half], db_s.at[s], db_r.at[half], across)

    third(0)
    third(1)

    def forward(u, carried):
        s, t = u // 8, u % 8
        row = (r + 2 * ROWS - z - 1 - t) % ROWS
        hl = (yl + s) % 2
        wait_copy(rr_in.at[row, hl], rr_r.at[row * 2 + hl])

        @pl.when(row != z)
        def _():
            zr_copy(row, hl).start()
        return carried

    lax.fori_loop(0, 16, forward, 0)

    near = pl.ds(pl.multiple_of(yl * HALF + core * BLOCK, BLOCK), BLOCK)
    far = pl.ds(pl.multiple_of(yl * HALF + (1 - core) * BLOCK, BLOCK), BLOCK)
    turned = flip(db_acc[:, far]).astype(BF16)
    for half in range(2):
        dbo_out[half] = turned[:, half * HALF:(half + 1) * HALF]
    twin = core * 2 + 1 - yl

    def dbo_copy():
        return remote(dbo_out, rest.at[head], db_s.at[2], db_r.at[2], other)

    def dbt_copy(half):
        return remote(
            dby_in.at[half, 1 - core], rest.at[twin, half], db_s.at[3 + half], db_r.at[3 + half], other)

    dbo_copy().start()
    own_ref[...] = flip(db_acc[:, near])
    for s in range(2):
        half = (yl + 1 + s) % 2
        wait_copy(dby_in.at[half], db_r.at[half])
        dbt_copy(half).start()

    total = jnp.zeros((2, HEAD_DIM, HALF), F32)
    wait_copy(dq_in, dq_r)
    for row in range(ROWS):
        total += dq_in[row].astype(F32)

    def hand_over(slot, total):
        low, high = total[:, :, :BLOCK], total[:, :, BLOCK:]
        mine = jnp.where(core == 0, low, high)
        fx_out[slot] = jnp.where(core == 0, high, low)
        grads_ref[slot, core] = mine

    def fx_copy(start, size):
        part = pl.ds(start, size)
        return remote(fx_out.at[part], fx_in.at[part], fx_s.at[start], fx_r.at[start], other)

    hand_over(0, total)
    fx_copy(0, 1).start()

    rest_ref[twin] = dby_in[:, core]
    wait_copy(rest.at[2 * (1 - core) + yl], db_r.at[2])
    for half in range(2):
        wait_copy(rest.at[2 * (1 - core) + 1 - yl, half], db_r.at[3 + half])
    for y in range(2):
        rest_ref[2 * (1 - core) + y] = rest[2 * (1 - core) + y]
    rest_ref[head] = jnp.zeros((2, BLOCK, HALF), BF16)
    wait_copy(fx_in.at[pl.ds(0, 1)], fx_r.at[0])
    grads_ref[0, 1 - core] = fx_in[0]

    total = rr_in[z].astype(F32)
    for d in (1, 7, 2, 6, 3, 5, 4):
        plane = (z + d) % PLANES
        wait_copy(zr_in.at[plane], zr_r.at[plane])
        total += zr_in[plane].astype(F32)
    hand_over(1, total[:, 0])
    hand_over(2, total[:, 1])
    fx_copy(1, 2).start()

    for kind in (K, Q, V, G):
        swap_copy(kind).wait_send()
        if kind in (Q, G):
            drained(48, in_s.at[kind])
            drained(192, tree_s.at[kind])
        else:
            kv_sent(kind)
    bias_core().wait_send()
    bias_near().wait_send()
    bias_far().wait_send()
    for part in range(2):
        wait_copy(st.at[part, pl.ds(0, ROWS - 1)], st_s.at[part])
    drained(480, rr_s)
    drained(448, zr_s)
    drained(240, dq_s)
    for s in range(2):
        dby_copy(s, (yl + s) % 2).wait_send()
        dbt_copy(s).wait_send()
    dbo_copy().wait_send()
    fx_copy(0, 1).wait_send()
    fx_copy(1, 2).wait_send()
    wait_copy(fx_in.at[pl.ds(1, 2)], fx_r.at[1])
    for slot in (1, 2):
        grads_ref[slot, 1 - core] = fx_in[slot]


def finish(grads_ref, own_ref, rest_ref, dq_ref, dk_ref, dv_ref, db_ref):
    c = lax.axis_index("col")
    head = (c % 2) * 2 + (c // 2) % 2
    for slot, ref, scale in ((0, dq_ref, SCALE), (1, dk_ref, SCALE), (2, dv_ref, None)):
        turned = jnp.transpose(grads_ref[slot].reshape(BLOCK, BLOCK))
        ref[0] = turned if scale is None else turned * scale
    for h in range(HEADS):
        for half in range(2):
            db_ref[h, :, half * HALF:(half + 1) * HALF] = rest_ref[h, half].astype(F32)
    db_ref[head] = own_ref[...]


def on_device(query_pair, key_pair, value_pair, pair_bias, residue_mask, grad_output):
    dma = pltpu.SemaphoreType.DMA
    vm = pltpu.VMEM
    scratch = [
        vm((4, 2, 2, HEAD_DIM, BLOCK), BF16),
        vm((4, 2, HEAD_DIM, BLOCK), BF16),
        vm((4, ROWS, 2, 2, HEAD_DIM, BLOCK), BF16),
        vm((ROWS, WIDE, HEAD_DIM), BF16),
        vm((2, BLOCK, WIDE), BF16),
        vm((2, 2, BLOCK, WIDE), BF16),
        vm((WIDE, WIDE), F32),
        vm((WIDE, WIDE), F32),
        vm((ROWS, WIDE, WIDE), F32),
        vm((ROWS, WIDE, WIDE), F32),
        vm((3, ROWS, CHUNKS, LINES, WIDE), F32),
        vm((2, ROWS, 2, ROWS, HALF), F32),
        vm((ROWS, CHUNKS + 1, LINES, WIDE), F32),
        vm((2, HALF, WIDE), BF16),
        vm((2, HALF, WIDE), BF16),
        vm((2 * ROWS, 2, HEAD_DIM, HALF), BF16),
        vm((ROWS, 2, 2, HEAD_DIM, HALF), BF16),
        vm((PLANES, 2, 2, HEAD_DIM, HALF), BF16),
        vm((ROWS, HEAD_DIM, WIDE), F32),
        vm((2 * ROWS, HEAD_DIM, HALF), BF16),
        vm((ROWS, 2, HEAD_DIM, HALF), BF16),
        vm((3, 2, HEAD_DIM, BLOCK), F32),
        vm((3, 2, HEAD_DIM, BLOCK), F32),
        vm((2, 2, BLOCK, HALF), BF16),
        vm((2, 2, BLOCK, HALF), BF16),
        vm((2, BLOCK, HALF), BF16),
        vm((HEADS, 2, BLOCK, HALF), BF16),
        dma((4,)), dma((4,)), dma((4,)), dma((4, 8)), dma((4,)), dma((3,)), dma((3,)),
        dma((2,)), dma((2,)), dma, dma((16,)), dma, dma((8,)),
        dma, dma, dma((2,)), dma((2,)), dma((5,)), dma((5,)),
    ]
    vmem = pl.BlockSpec(memory_space=pltpu.VMEM)
    shape = jax.ShapeDtypeStruct
    parts = pl.pallas_call(
        kernel,
        out_shape=(
            shape((3, 2, 2, HEAD_DIM, BLOCK), F32),
            shape((BLOCK, WIDE), F32),
            shape((HEADS, 2, BLOCK, HALF), BF16),
        ),
        in_specs=[vmem] * 6,
        out_specs=(vmem,) * 3,
        scratch_shapes=scratch,
        compiler_params=pltpu.CompilerParams(
            collective_id=0, has_side_effects=True, vmem_limit_bytes=56 * 1024 * 1024),
        cost_estimate=pl.CostEstimate(flops=4_000_000_000, bytes_accessed=3_000_000, transcendentals=2_200_000),
    )(query_pair, key_pair, value_pair, pair_bias, residue_mask.reshape(1, -1), grad_output)
    pair = shape((1, BLOCK, BLOCK), F32)
    return pl.pallas_call(
        finish,
        out_shape=(pair, pair, pair, shape((HEADS, BLOCK, WIDE), F32)),
        in_specs=[vmem] * 3,
        out_specs=(vmem,) * 4,
        compiler_params=pltpu.CompilerParams(vmem_limit_bytes=60 * 1024 * 1024),
        cost_estimate=pl.CostEstimate(flops=1_000_000, bytes_accessed=2_500_000, transcendentals=0),
    )(*parts)


def solution(mesh):
    in_specs = (
        P("row", "col", None),
        P("row", "col", None),
        P("row", "col", None),
        P(None, "col", "row"),
        P("row"),
        P("row", "col", None),
    )
    out_specs = (
        P("row", "col", None),
        P("row", "col", None),
        P("row", "col", None),
        P(None, "col", "row"),
    )
    return jax.shard_map(
        on_device, mesh=mesh, in_specs=in_specs, out_specs=out_specs, check_vma=False
    )
```
